256 devices in a mesh: ctx: 32 (over z, x), tp: 8 (over y, core).
Axes of the slice: x: 4, y: 4, z: 8, core: 2. Of those that a mesh axis runs over, the one named last changes fastest.
Arguments:
- queries: bfloat16 [16384, 4096], P('ctx', 'tp'), may hold values from -90 to 90
- key_states: bfloat16 [16384, 1024], P('ctx', 'tp'), may hold values from -3 to 3
- values: bfloat16 [16384, 1024], P('ctx', 'tp'), may hold values from -6 to 6
- out_grad: bfloat16 [16384, 4096], P('ctx', 'tp'), may hold values from -6 to 6
- weight: bfloat16 [4096, 6144], P(None, 'tp'), may hold values from -0.09375 to 0.09375
- lengths: int32 [64], replicated, may hold values from 128 to 384, as said below
- block_plan: int32 [128], replicated, may hold values from 0 to 31, as said below
Outputs:
- attention_out: bfloat16 [16384, 4096], P('ctx', 'tp')
- grad_input: bfloat16 [16384, 4096], P('ctx', 'tp')
- log_sum_exp: float32 [32, 16384], P('tp', 'ctx')
The draws below stay inside these ranges and needn't reach their ends.
Inputs may be any that keep to these rules, and one draw needn't show every extreme that they name: `lengths`: the documents lie end to end in window order and together hold 16384 tokens; every length is a whole number of blocks of 128 tokens, so documents begin and end at block bounds. `block_plan`: entry b is the device of ctx that block b of the window (tokens b * 128 to b * 128 + 127) goes to. All blocks of one document go to one device, and every device receives exactly 4 blocks. A block goes to the device that holds it in the window or to the next or previous index of ctx (no wrap). A device sends at most 3 blocks to each of its two neighbours, and in every draw some device sends 3 blocks to the next index.
All inputs are finite; a program needn't handle non-finite values.
Results may differ from the reference program's by a relative error of at most 0.033.
Values may be sent and summed in bfloat16 or wider, within the bound.
A program may use at most 64 MiB of HBM per device.

```python
import jax
import jax.numpy as jnp
from jax import lax

D = 4096
HEADS = 32
KV_HEADS = 8
HEAD_DIM = 128
BLOCK = 128
TOK_DEV = 512
GROUP = 4
QKV = 6144
SLAB = 768
BLOCKS_DEV = 4
REACH = 256
TOKENS = 16384
NBLOCKS = 128
N_CTX = 32
N_TP = 8


def window_keys(key):
    base = jax.random.normal(jax.random.fold_in(key, 101), (TOKENS, KV_HEADS * HEAD_DIM), jnp.float32)
    base = jnp.clip(base, -3.0, 3.0)
    return base


def doc_blocks(key):
    shards = TOKENS // TOK_DEV
    sizes = jax.random.randint(jax.random.fold_in(key, 111), (shards,), 1, BLOCKS_DEV)
    centre = jax.random.randint(jax.random.fold_in(key, 112), (), 1, shards - 1)
    index = jnp.arange(shards, dtype=jnp.int32)
    sizes = jnp.where((index == centre - 1) | (index == centre), 1, sizes)
    sizes = jnp.where(index == centre + 1, BLOCKS_DEV - 1, sizes)
    rest = BLOCKS_DEV - sizes
    middle = jnp.stack([sizes[1:], rest[:-1]], axis=1).reshape(-1)
    return jnp.concatenate([sizes[:1], middle, rest[-1:]]).astype(jnp.int32)


def draw_queries(key, part):
    key = jax.random.fold_in(key, 2)
    fresh = jax.random.normal(key, (TOKENS, HEADS * HEAD_DIM), jnp.float32)
    return fresh.astype(jnp.bfloat16)


def draw_key_states(key, part):
    base = window_keys(key)
    return base.astype(jnp.bfloat16)


def draw_lengths(key, part):
    counts = doc_blocks(key)
    return (counts * BLOCK).astype(jnp.int32)


def draw_block_plan(key, part):
    counts = doc_blocks(key)
    shards = TOKENS // TOK_DEV
    ends = jnp.cumsum(counts)
    index = jnp.arange(NBLOCKS, dtype=jnp.int32)
    which = jnp.sum((index[:, None] >= ends[None, :]).astype(jnp.int32), axis=1).astype(jnp.int32)
    odd_dest = jnp.minimum((which + 1) // 2, shards - 1)
    even_dest = jnp.maximum(which // 2 - 1, 0)
    return jnp.where(which % 2 == 1, odd_dest, even_dest).astype(jnp.int32)


def levels(stream_key, extent, pieces, least, high):
    loudness = 1.0
    for dim, shards_of in pieces:
        heights = jax.random.uniform(jax.random.fold_in(jax.random.fold_in(stream_key, 6), dim), (shards_of,), jnp.float32, least / len(pieces), high / len(pieces))
        loudness = loudness * jnp.repeat(jnp.exp(heights), extent[dim] // shards_of).reshape((-1,) + (1,) * (len(extent) - 1 - dim))
    return loudness


def centred(own_key, shape, width, limit, pieces=(), held_as=jnp.bfloat16):
    gain = levels(own_key, shape, pieces, -0.22, 0.18) if pieces else 1.0
    entries = jax.random.normal(own_key, shape, jnp.float32) * width * gain
    return jnp.minimum(jnp.maximum(entries, -limit), limit).astype(held_as)


def setup_inputs(seed: int = 0) -> dict:
    arg_keys = jax.random.split(jax.random.key(seed), 8)
    queries = draw_queries(jax.random.fold_in(arg_keys[7], 71), 0)
    key_states = draw_key_states(jax.random.fold_in(arg_keys[7], 71), 0)
    values = centred(arg_keys[2], (TOKENS, KV_HEADS * HEAD_DIM), 1.0, 6.0, ((0, 32), (1, 8)))
    out_grad = centred(arg_keys[3], (TOKENS, HEADS * HEAD_DIM), 1.0, 6.0, ((0, 32), (1, 8)))
    weight = centred(arg_keys[4], (D, QKV), D ** -0.5, 0.09375, ((1, 8),))
    lengths = draw_lengths(jax.random.fold_in(arg_keys[7], 71), 0)
    block_plan = draw_block_plan(jax.random.fold_in(arg_keys[7], 71), 0)
    return {"queries": queries, "key_states": key_states, "values": values, "out_grad": out_grad, "weight": weight, "lengths": lengths, "block_plan": block_plan}


def rounded(array):
    return lax.optimization_barrier(array.astype(jnp.bfloat16)).astype(jnp.float32)


def doc_index(lengths, positions):
    bounds = jnp.cumsum(lengths)
    return jnp.sum((positions[:, None] >= bounds[None, :]).astype(jnp.int32), axis=1).astype(jnp.int32)


def attend(query_part, key_heads, value_heads, grad_part, query_pos, query_doc, key_pos, key_doc):
    scale = HEAD_DIM ** -0.5
    query_f = query_part.astype(jnp.float32)
    key_f = key_heads.astype(jnp.float32)
    value_f = value_heads.astype(jnp.float32)
    grad_f = grad_part.astype(jnp.float32)
    scores = jnp.einsum("qgjd,kgd->gjqk", query_f, key_f) * scale
    allowed = (query_doc[:, None] == key_doc[None, :]) & (key_pos[None, :] <= query_pos[:, None]) & (key_pos[None, :] >= 0)
    scores = jnp.where(allowed, scores, -jnp.inf)
    top = jnp.max(scores, axis=-1, keepdims=True)
    raised = jnp.exp(scores - top)
    row_sum = jnp.sum(raised, axis=-1, keepdims=True)
    weights = raised / row_sum
    row_lse = (top + jnp.log(row_sum))[..., 0]
    weights_low = rounded(weights)
    result_wide = jnp.einsum("gjqk,kgd->qgjd", weights_low, value_f)
    result = result_wide.astype(jnp.bfloat16)
    result_f = rounded(result_wide)
    row_dot = jnp.sum(grad_f * result_f, axis=-1)
    prob_grad = jnp.einsum("qgjd,kgd->gjqk", grad_f, value_f)
    score_grad = rounded(weights * (prob_grad - jnp.transpose(row_dot, (1, 2, 0))[..., None]) * scale)
    query_grad = jnp.einsum("gjqk,kgd->qgjd", score_grad, key_f).astype(jnp.bfloat16)
    key_grad = jnp.einsum("gjqk,qgjd->kgd", score_grad, query_f)
    value_grad = jnp.einsum("gjqk,qgjd->kgd", weights_low, grad_f)
    return result, row_lse, query_grad, key_grad, value_grad


def reference(queries, key_states, values, out_grad, weight, lengths, block_plan):
    query_split = queries.reshape(N_CTX, TOK_DEV, KV_HEADS, GROUP, HEAD_DIM)
    grad_split = out_grad.reshape(N_CTX, TOK_DEV, KV_HEADS, GROUP, HEAD_DIM)
    key_padded = jnp.concatenate([jnp.zeros((REACH, KV_HEADS * HEAD_DIM), key_states.dtype), key_states], 0)
    value_padded = jnp.concatenate([jnp.zeros((REACH, KV_HEADS * HEAD_DIM), values.dtype), values], 0)
    shard_ids = jnp.arange(N_CTX, dtype=jnp.int32)

    def one_shard(item):
        query_part, grad_part, shard = item
        first = (shard * TOK_DEV).astype(jnp.int32)
        query_pos = first + jnp.arange(TOK_DEV, dtype=jnp.int32)
        key_pos = first - REACH + jnp.arange(TOK_DEV + REACH, dtype=jnp.int32)
        key_part = lax.dynamic_slice_in_dim(key_padded, first, TOK_DEV + REACH, 0).reshape(TOK_DEV + REACH, KV_HEADS, HEAD_DIM)
        value_part = lax.dynamic_slice_in_dim(value_padded, first, TOK_DEV + REACH, 0).reshape(TOK_DEV + REACH, KV_HEADS, HEAD_DIM)
        return attend(query_part, key_part, value_part, grad_part, query_pos, doc_index(lengths, query_pos), key_pos, doc_index(lengths, key_pos))

    result, row_lse, query_grad, key_grad, value_grad = lax.map(one_shard, (query_split, grad_split, shard_ids))
    attention_out = result.reshape(TOKENS, HEADS * HEAD_DIM)

    def settle(grads):
        own = grads[:, REACH:]
        spill = jnp.concatenate([grads[1:, :REACH], jnp.zeros_like(grads[:1, :REACH])], 0)
        own = own.at[:, TOK_DEV - REACH:].add(spill)
        return own.reshape(TOKENS, KV_HEADS, HEAD_DIM).astype(jnp.bfloat16)

    key_total = settle(key_grad)
    value_total = settle(value_grad)
    stacked = jnp.concatenate([query_grad.reshape(TOKENS, KV_HEADS, GROUP * HEAD_DIM), key_total, value_total], 2).reshape(TOKENS, QKV)
    stacked_slabs = stacked.reshape(TOKENS, N_TP, SLAB).transpose(1, 0, 2)
    weight_slabs = weight.reshape(D, N_TP, SLAB).transpose(1, 0, 2)

    def add_slab(total, pair):
        part = jnp.dot(pair[0], pair[1].T, preferred_element_type=jnp.float32)
        return total + rounded(part), None

    total = lax.scan(add_slab, jnp.zeros((TOKENS, D), jnp.float32), (stacked_slabs, weight_slabs))[0]
    grad_input = total.astype(jnp.bfloat16)
    lse_all = jnp.transpose(row_lse, (1, 2, 0, 3)).reshape(HEADS, TOKENS)
    order = jnp.argsort(block_plan, stable=True).astype(jnp.int32)
    token_order = (order[:, None] * BLOCK + jnp.arange(BLOCK, dtype=jnp.int32)[None, :]).reshape(-1)
    log_sum_exp = lse_all[:, token_order]
    return attention_out, grad_input, log_sum_exp
```

```python
import jax
import jax.numpy as jnp
from jax import lax
from jax.experimental import pallas as pl
from jax.experimental.pallas import tpu as pltpu
from jax.sharding import PartitionSpec as P

HEAD_DIM = 128
BLOCK = 128
GROUP = 4
BLOCKS = 4
REACH_BLOCKS = 2
NEG = -1e30
LOG2E = 1.4426950408889634
MESH = pl.DeviceIdType.MESH
F32 = jnp.float32
BF16 = jnp.bfloat16


def dot(a, b, dims):
    return lax.dot_general(a, b, (dims, ((), ())), preferred_element_type=F32)


def remote(src, dst, send, recv, device):
    return pltpu.make_async_remote_copy(
        src_ref=src,
        dst_ref=dst,
        send_sem=send,
        recv_sem=recv,
        device_id=device,
        device_id_type=MESH,
    )


def kernel(
    q_ref, k_ref, v_ref, g_ref, w_ref, len_ref, plan_ref,
    o_ref, gi_ref, lse_ref,
    kbuf, vbuf, qbuf, gbuf, wown, wpar, dkv, ret, st,
    s2, sp, sm, hp, hm, rp, rm, own, mp, mm,
    obuf, gibuf, lbuf, lout,
    lsem, wsem, osem,
    halo_s, halo_r, w_s, w_r, st_s, st_r, ret_s, ret_r, lse_s, lse_r, rs_s, rs_r,
):
    n_ctx = lax.axis_size("ctx")
    n_tp = lax.axis_size("tp")
    n_y = n_tp // 2
    ctx = lax.axis_index("ctx")
    tp = lax.axis_index("tp")
    y = tp // 2
    core = tp - 2 * y
    nxt = {"ctx": lax.rem(ctx + 1, n_ctx)}
    prv = {"ctx": lax.rem(ctx + n_ctx - 1, n_ctx)}
    par = {"tp": tp + 1 - 2 * core}
    up = {"tp": lax.rem(tp + 2, n_tp)}
    dn = {"tp": lax.rem(tp + n_tp - 2, n_tp)}

    barrier = pltpu.get_barrier_semaphore()
    for device in (nxt, prv, par, up, dn):
        pl.semaphore_signal(barrier, inc=1, device_id=device, device_id_type=MESH)

    locals_ = [
        pltpu.make_async_copy(k_ref, kbuf.at[pl.ds(256, 512)], lsem.at[0]),
        pltpu.make_async_copy(q_ref, qbuf, lsem.at[1]),
        pltpu.make_async_copy(v_ref, vbuf.at[pl.ds(256, 512)], lsem.at[2]),
        pltpu.make_async_copy(g_ref, gbuf, lsem.at[3]),
    ]
    for copy in locals_:
        copy.start()

    def w_rows(r, c):
        return pl.ds(pl.multiple_of((2 * lax.rem(y + r, n_y) + c) * 512, 512), 512)

    w_local = [
        pltpu.make_async_copy(w_ref.at[w_rows(r, core)], wown.at[r], wsem.at[r])
        for r in range(4)
    ]
    for r in (2, 1, 3, 0):
        w_local[r].start()

    first = ctx * BLOCKS

    def scan_lengths(i, carry):
        total = carry[0] + len_ref[i]
        return (total,) + tuple(
            carry[1 + b] + jnp.where(total == (first + b - 1) * BLOCK, 1, 0)
            for b in range(5)
        )

    start = jnp.int32(0)
    edge = jnp.where(ctx == 0, 1, 0).astype(jnp.int32)
    found = lax.fori_loop(
        0, len_ref.shape[0], scan_lengths, (start, start, edge, start, start, start)
    )[1:]

    pl.semaphore_wait(barrier, 5)

    halo = {}
    slot = 0
    for b in (1, 0):
        for src, dst in ((k_ref, kbuf), (v_ref, vbuf)):
            copy = remote(
                src.at[pl.ds(256 + b * BLOCK, BLOCK)],
                dst.at[pl.ds(b * BLOCK, BLOCK)],
                halo_s.at[slot], halo_r.at[slot], nxt,
            )
            copy.start()
            halo.setdefault(b, []).append(copy)
            slot += 1
    w_swap = [
        remote(w_ref.at[w_rows(r, 1 - core)], wpar.at[r], w_s.at[r], w_r.at[r], par)
        for r in range(4)
    ]
    for r in (2, 1, 3, 0):
        w_swap[r].start()

    for copy in locals_:
        copy.wait()

    scale = HEAD_DIM ** -0.5
    causal = lax.broadcasted_iota(jnp.int32, (BLOCK, BLOCK), 0) <= lax.broadcasted_iota(
        jnp.int32, (BLOCK, BLOCK), 1
    )
    causal_bias = jnp.where(causal, 0.0, NEG).astype(F32)
    causal_bias = jnp.concatenate([causal_bias] * GROUP, axis=1)
    written = set()

    def add_grad(which, index, value):
        rows = pl.ds(index * BLOCK, BLOCK)
        if (which, index) in written:
            dkv[which, rows, :] += value
        else:
            written.add((which, index))
            dkv[which, rows, :] = value

    def heads_in_rows(ref, qb):
        rows = pl.ds(qb * BLOCK, BLOCK)
        return jnp.concatenate(
            [ref[rows, pl.ds(h * HEAD_DIM, HEAD_DIM)] for h in range(GROUP)], axis=0
        )

    def attend(qb):
        rows = pl.ds(qb * BLOCK, BLOCK)
        keys = kbuf[pl.ds(qb * BLOCK, 3 * BLOCK), :]
        vals = vbuf[pl.ds(qb * BLOCK, 3 * BLOCK), :]
        queries = heads_in_rows(qbuf, qb)
        grads = heads_in_rows(gbuf, qb)
        near = jnp.where(found[qb + 1] > 0, NEG, 0.0).astype(F32)
        far = jnp.where(found[qb + 1] + found[qb] > 0, NEG, 0.0).astype(F32)
        scores = dot(keys, queries, ((1,), (1,)))
        prob = dot(vals, grads, ((1,), (1,)))
        scores = jnp.concatenate(
            [
                scores[:BLOCK] + far,
                scores[BLOCK : 2 * BLOCK] + near,
                scores[2 * BLOCK :] + causal_bias,
            ],
            axis=0,
        )
        top = jnp.max(scores, axis=0, keepdims=True)
        raised = jnp.exp2((scores - top) * (scale * LOG2E))
        total = jnp.sum(raised, axis=0, keepdims=True)
        mixed = jnp.sum(raised * prob, axis=0, keepdims=True)
        inverse = 1.0 / total
        row_dot = mixed * inverse
        lse = top * scale + jnp.log(total)
        for h in range(GROUP):
            lbuf[0, pl.ds(h, 1), rows] = lse[:, h * BLOCK : (h + 1) * BLOCK]
        weights = raised * inverse
        weights_low = weights.astype(BF16)
        score_grad = (weights * (prob - row_dot)).astype(BF16)
        out = dot(vals, weights_low, ((0,), (0,))).astype(BF16)
        query_grad = (dot(keys, score_grad, ((0,), (0,))) * scale).astype(BF16)
        for h in range(GROUP):
            columns = slice(h * BLOCK, (h + 1) * BLOCK)
            obuf[rows, pl.ds(h * HEAD_DIM, HEAD_DIM)] = out[:, columns].T
            st[0, qb, :, pl.ds(h * HEAD_DIM, HEAD_DIM)] = query_grad[:, columns].T
        key_add = dot(score_grad, queries, ((1,), (0,)))
        value_add = dot(weights_low, grads, ((1,), (0,)))
        for b in range(3):
            part = slice(b * BLOCK, (b + 1) * BLOCK)
            add_grad(0, qb + b, key_add[part])
            add_grad(1, qb + b, value_add[part])

    st_swap = [
        remote(st.at[0, t], st.at[1, t], st_s.at[t], st_r.at[t], par) for t in range(BLOCKS)
    ]

    def finish_tokens(t):
        rows = pl.ds((t + REACH_BLOCKS) * BLOCK, BLOCK)
        key_grad = dkv[0, rows, :]
        value_grad = dkv[1, rows, :]
        if t >= 2:
            back = pl.ds((t - 2) * BLOCK, BLOCK)
            key_grad = key_grad + ret[0, back, :]
            value_grad = value_grad + ret[1, back, :]
        st[0, t, :, pl.ds(GROUP * HEAD_DIM, HEAD_DIM)] = (key_grad * scale).astype(BF16)
        st[0, t, :, pl.ds((GROUP + 1) * HEAD_DIM, HEAD_DIM)] = value_grad.astype(BF16)
        st_swap[t].start()

    attend(2)
    attend(3)
    for copy in halo[1]:
        copy.wait_recv()
    attend(1)
    finish_tokens(1)
    for copy in halo[0]:
        copy.wait_recv()
    attend(0)
    finish_tokens(0)

    back_copy = remote(dkv.at[:, pl.ds(0, 256), :], ret, ret_s, ret_r, prv)
    back_copy.start()
    lse_next = remote(lbuf.at[0], lbuf.at[1], lse_s.at[0], lse_r.at[0], nxt)
    lse_prev = remote(lbuf.at[0], lbuf.at[2], lse_s.at[1], lse_r.at[1], prv)
    lse_next.start()
    lse_prev.start()
    out_copy = pltpu.make_async_copy(obuf, o_ref, osem.at[0])
    out_copy.start()

    HALF = BLOCK // 2
    lo, hi = pl.ds(0, HALF), pl.ds(HALF, HALF)
    for r in range(4):
        w_local[r].wait()

    sends = {}
    for t in range(BLOCKS):
        sends[t] = dict(
            h_up=remote(s2.at[t, lo], hp.at[t], rs_s.at[t, 0], rs_r.at[t, 0], up),
            h_dn=remote(s2.at[t, hi], hm.at[t], rs_s.at[t, 1], rs_r.at[t, 1], dn),
            u_up=remote(sp.at[t, hi], rp.at[t, hi], rs_s.at[t, 2], rs_r.at[t, 2], up),
            u_dn=remote(sm.at[t, lo], rm.at[t, lo], rs_s.at[t, 3], rs_r.at[t, 3], dn),
            m_up=remote(sp.at[t, lo], rp.at[t, lo], rs_s.at[t, 4], rs_r.at[t, 4], up),
            m_dn=remote(sm.at[t, hi], rm.at[t, hi], rs_s.at[t, 5], rs_r.at[t, 5], dn),
        )

    def project(t, first_time):
        st_swap[t].wait_recv()

        def part(r):
            if first_time:
                w_swap[r].wait_recv()
            return dot(st[0, t], wown[r], ((1,), (1,))) + dot(st[1, t], wpar[r], ((1,), (1,)))

        s2[t] = part(2).astype(BF16)
        sends[t]["h_up"].start()
        sends[t]["h_dn"].start()
        piece = part(1)
        sp[t, hi, :] = piece[HALF:].astype(BF16)
        sends[t]["u_up"].start()
        mp[t] = piece[:HALF]
        piece = part(3)
        sm[t, lo, :] = piece[:HALF].astype(BF16)
        sends[t]["u_dn"].start()
        mm[t] = piece[HALF:]
        own[t] = part(0)

    def merge(t):
        sends[t]["h_up"].wait_recv()
        sp[t, lo, :] = (mp[t] + hp[t].astype(F32)).astype(BF16)
        sends[t]["m_up"].start()
        sends[t]["h_dn"].wait_recv()
        sm[t, hi, :] = (mm[t] + hm[t].astype(F32)).astype(BF16)
        sends[t]["m_dn"].start()

    gi_copies = []

    def finish(t):
        for name in ("u_up", "u_dn", "m_up", "m_dn"):
            sends[t][name].wait_recv()
        rows = pl.ds(t * BLOCK, BLOCK)
        gibuf[rows, :] = (own[t] + rp[t].astype(F32) + rm[t].astype(F32)).astype(BF16)
        copy = pltpu.make_async_copy(gibuf.at[rows], gi_ref.at[rows], osem.at[1 + t])
        copy.start()
        gi_copies.append(copy)

    project(1, True)
    project(0, False)
    back_copy.wait_recv()
    finish_tokens(2)
    finish_tokens(3)
    merge(1)
    project(2, False)
    merge(0)
    project(3, False)
    merge(2)

    lse_next.wait_recv()
    lse_prev.wait_recv()
    picked = [jnp.zeros((GROUP, BLOCK), F32) for _ in range(BLOCKS)]
    rank = jnp.int32(0)
    for source, device in ((1, prv["ctx"]), (0, ctx), (2, nxt["ctx"])):
        for b in range(BLOCKS):
            hit = jnp.where(plan_ref[device * BLOCKS + b] == ctx, 1, 0)
            piece = lbuf[source, :, pl.ds(b * BLOCK, BLOCK)]
            for s in range(BLOCKS):
                take = jnp.where((hit == 1) & (rank == s), 1.0, 0.0).astype(F32)
                picked[s] = picked[s] + piece * take
            rank = rank + hit
    for s in range(BLOCKS):
        lout[:, pl.ds(s * BLOCK, BLOCK)] = picked[s]
    lse_copy = pltpu.make_async_copy(lout, lse_ref, osem.at[5])
    lse_copy.start()

    merge(3)
    for t in (1, 0, 2, 3):
        finish(t)

    out_copy.wait()
    lse_copy.wait()
    for copy in gi_copies:
        copy.wait()
    for b in (1, 0):
        for copy in halo[b]:
            copy.wait_send()
    for copy in w_swap:
        copy.wait_send()
    for copy in st_swap:
        copy.wait_send()
    back_copy.wait_send()
    lse_next.wait_send()
    lse_prev.wait_send()
    for t in range(BLOCKS):
        for copy in sends[t].values():
            copy.wait_send()


def body(queries, key_states, values, out_grad, weight, lengths, block_plan):
    anywhere = pl.BlockSpec(memory_space=pl.ANY)
    scalars = pl.BlockSpec(memory_space=pltpu.SMEM)
    dma = pltpu.SemaphoreType.DMA
    return pl.pallas_call(
        kernel,
        out_shape=(
            jax.ShapeDtypeStruct((512, 512), BF16),
            jax.ShapeDtypeStruct((512, 512), BF16),
            jax.ShapeDtypeStruct((GROUP, 512), F32),
        ),
        in_specs=[anywhere] * 5 + [scalars] * 2,
        out_specs=(anywhere,) * 3,
        scratch_shapes=[
            pltpu.VMEM((768, 128), BF16),
            pltpu.VMEM((768, 128), BF16),
            pltpu.VMEM((512, 512), BF16),
            pltpu.VMEM((512, 512), BF16),
            pltpu.VMEM((4, 512, 768), BF16),
            pltpu.VMEM((4, 512, 768), BF16),
            pltpu.VMEM((2, 768, 128), F32),
            pltpu.VMEM((2, 256, 128), F32),
            pltpu.VMEM((2, 4, 128, 768), BF16),
            pltpu.VMEM((4, 128, 512), BF16),
            pltpu.VMEM((4, 128, 512), BF16),
            pltpu.VMEM((4, 128, 512), BF16),
            pltpu.VMEM((4, 64, 512), BF16),
            pltpu.VMEM((4, 64, 512), BF16),
            pltpu.VMEM((4, 128, 512), BF16),
            pltpu.VMEM((4, 128, 512), BF16),
            pltpu.VMEM((4, 128, 512), F32),
            pltpu.VMEM((4, 64, 512), F32),
            pltpu.VMEM((4, 64, 512), F32),
            pltpu.VMEM((512, 512), BF16),
            pltpu.VMEM((512, 512), BF16),
            pltpu.VMEM((3, GROUP, 512), F32),
            pltpu.VMEM((GROUP, 512), F32),
            dma((4,)),
            dma((4,)),
            dma((6,)),
            dma((4,)), dma((4,)),
            dma((4,)), dma((4,)),
            dma((4,)), dma((4,)),
            dma, dma,
            dma((2,)), dma((2,)),
            dma((4, 6)), dma((4, 6)),
        ],
        compiler_params=pltpu.CompilerParams(
            collective_id=0, has_side_effects=True, vmem_limit_bytes=44 * 1024 * 1024
        ),
    )(queries, key_states, values, out_grad, weight, lengths, block_plan)


def solution(mesh):
    in_specs = (
        P("ctx", "tp"),
        P("ctx", "tp"),
        P("ctx", "tp"),
        P("ctx", "tp"),
        P(None, "tp"),
        P(),
        P(),
    )
    out_specs = (P("ctx", "tp"), P("ctx", "tp"), P("tp", "ctx"))
    return jax.shard_map(body, mesh=mesh, in_specs=in_specs, out_specs=out_specs, check_vma=False)
```

```python
import jax
import jax.numpy as jnp
from jax import lax
from jax.experimental import pallas as pl
from jax.experimental.pallas import tpu as pltpu
from jax.sharding import PartitionSpec as P

HEAD_DIM = 128
BLOCK = 128
GROUP = 4
BLOCKS = 4
REACH_BLOCKS = 2
NEG = -1e30
VMEM_LIMIT = 60 * 1024 * 1024
LOG2E = 1.4426950408889634
MESH = pl.DeviceIdType.MESH
F32 = jnp.float32
BF16 = jnp.bfloat16


def dot(a, b, dims):
    return lax.dot_general(a, b, (dims, ((), ())), preferred_element_type=F32)


def remote(src, dst, send, recv, device):
    return pltpu.make_async_remote_copy(
        src_ref=src,
        dst_ref=dst,
        send_sem=send,
        recv_sem=recv,
        device_id=device,
        device_id_type=MESH,
    )


def kernel(
    q_ref, k_ref, v_ref, g_ref, w_ref, len_hbm, plan_hbm,
    o_ref, gi_ref, lse_ref,
    kbuf, vbuf, qbuf, gbuf, wown, wpar, dkv, ret, st,
    s2, sp, sm, hp, hm, rp, rm, own, mp, mm,
    obuf, gibuf, lbuf, lout, len_ref, plan_ref,
    lsem, wsem, osem,
    halo_s, halo_r, w_s, w_r, st_s, st_r, ret_s, ret_r, lse_s, lse_r, rs_s, rs_r,
):
    n_ctx = lax.axis_size("ctx")
    n_tp = lax.axis_size("tp")
    n_y = n_tp // 2
    ctx = lax.axis_index("ctx")
    tp = lax.axis_index("tp")
    y = tp // 2
    core = tp - 2 * y
    nxt = {"ctx": lax.rem(ctx + 1, n_ctx)}
    prv = {"ctx": lax.rem(ctx + n_ctx - 1, n_ctx)}
    par = {"tp": tp + 1 - 2 * core}
    up = {"tp": lax.rem(tp + 2, n_tp)}
    dn = {"tp": lax.rem(tp + n_tp - 2, n_tp)}

    has_next = ctx < n_ctx - 1
    has_prev = ctx > 0

    def greet(device):
        pl.semaphore_signal(barrier, inc=1, device_id=device, device_id_type=MESH)

    barrier = pltpu.get_barrier_semaphore()
    pl.when(has_next)(lambda: greet(nxt))
    pl.when(has_prev)(lambda: greet(prv))
    for device in (par, up, dn):
        greet(device)
    len_copy = pltpu.make_async_copy(len_hbm, len_ref, lsem.at[4])
    plan_copy = pltpu.make_async_copy(plan_hbm, plan_ref, lsem.at[5])
    len_copy.start()
    plan_copy.start()

    locals_ = [
        pltpu.make_async_copy(k_ref, kbuf.at[pl.ds(256, 512)], lsem.at[0]),
        pltpu.make_async_copy(q_ref, qbuf, lsem.at[1]),
        pltpu.make_async_copy(v_ref, vbuf.at[pl.ds(256, 512)], lsem.at[2]),
        pltpu.make_async_copy(g_ref, gbuf, lsem.at[3]),
    ]
    for copy in locals_:
        copy.start()

    def w_rows(r, c):
        return pl.ds(pl.multiple_of((2 * lax.rem(y + r, n_y) + c) * 512, 512), 512)

    w_local = [
        pltpu.make_async_copy(w_ref.at[w_rows(r, core)], wown.at[r], wsem.at[r])
        for r in range(4)
    ]
    for r in (2, 1, 3, 0):
        w_local[r].start()

    def no_halo():
        kbuf[pl.ds(0, 256), :] = jnp.zeros((256, 128), BF16)
        vbuf[pl.ds(0, 256), :] = jnp.zeros((256, 128), BF16)
        lbuf[1] = jnp.zeros((GROUP, 512), F32)

    def no_return():
        ret[...] = jnp.zeros((2, 256, 128), F32)
        lbuf[2] = jnp.zeros((GROUP, 512), F32)

    pl.when(jnp.logical_not(has_prev))(no_halo)
    pl.when(jnp.logical_not(has_next))(no_return)

    first = ctx * BLOCKS

    def scan_lengths(i, carry):
        total = carry[0] + len_ref[i]
        return (total,) + tuple(
            carry[1 + b] + jnp.where(total == (first + b - 1) * BLOCK, 1, 0)
            for b in range(5)
        )

    start = jnp.int32(0)
    edge = jnp.where(ctx == 0, 1, 0).astype(jnp.int32)
    len_copy.wait()
    plan_copy.wait()
    found = lax.fori_loop(
        0, len_ref.shape[0], scan_lengths, (start, start, edge, start, start, start)
    )[1:]

    pl.semaphore_wait(
        barrier, 3 + jnp.where(has_next, 1, 0) + jnp.where(has_prev, 1, 0)
    )

    halo = {}
    slot = 0
    for b in (1, 0):
        for src, dst in ((k_ref, kbuf), (v_ref, vbuf)):
            copy = remote(
                src.at[pl.ds(256 + b * BLOCK, BLOCK)],
                dst.at[pl.ds(b * BLOCK, BLOCK)],
                halo_s.at[slot], halo_r.at[slot], nxt,
            )
            pl.when(has_next)(copy.start)
            halo.setdefault(b, []).append(copy)
            slot += 1
    w_swap = [
        remote(w_ref.at[w_rows(r, 1 - core)], wpar.at[r], w_s.at[r], w_r.at[r], par)
        for r in range(4)
    ]
    for r in (2, 1, 3, 0):
        w_swap[r].start()

    for copy in locals_:
        copy.wait()

    scale = HEAD_DIM ** -0.5
    causal = lax.broadcasted_iota(jnp.int32, (BLOCK, BLOCK), 0) <= lax.broadcasted_iota(
        jnp.int32, (BLOCK, BLOCK), 1
    )
    causal_bias = jnp.where(causal, 0.0, NEG).astype(F32)
    causal_bias = jnp.concatenate([causal_bias] * GROUP, axis=1)
    written = set()

    def add_grad(which, index, value):
        rows = pl.ds(index * BLOCK, BLOCK)
        if (which, index) in written:
            dkv[which, rows, :] += value
        else:
            written.add((which, index))
            dkv[which, rows, :] = value

    def heads_in_rows(ref, qb):
        rows = pl.ds(qb * BLOCK, BLOCK)
        return jnp.concatenate(
            [ref[rows, pl.ds(h * HEAD_DIM, HEAD_DIM)] for h in range(GROUP)], axis=0
        )

    def attend(qb):
        rows = pl.ds(qb * BLOCK, BLOCK)
        keys = kbuf[pl.ds(qb * BLOCK, 3 * BLOCK), :]
        vals = vbuf[pl.ds(qb * BLOCK, 3 * BLOCK), :]
        queries = heads_in_rows(qbuf, qb)
        grads = heads_in_rows(gbuf, qb)
        near = jnp.where(found[qb + 1] > 0, NEG, 0.0).astype(F32)
        far = jnp.where(found[qb + 1] + found[qb] > 0, NEG, 0.0).astype(F32)
        scores = dot(keys, queries, ((1,), (1,)))
        prob = dot(vals, grads, ((1,), (1,)))
        scores = jnp.concatenate(
            [
                scores[:BLOCK] + far,
                scores[BLOCK : 2 * BLOCK] + near,
                scores[2 * BLOCK :] + causal_bias,
            ],
            axis=0,
        )
        top = jnp.max(scores, axis=0, keepdims=True)
        raised = jnp.exp2((scores - top) * (scale * LOG2E))
        total = jnp.sum(raised, axis=0, keepdims=True)
        mixed = jnp.sum(raised * prob, axis=0, keepdims=True)
        inverse = 1.0 / total
        row_dot = mixed * inverse
        lse = top * scale + jnp.log(total)
        for h in range(GROUP):
            lbuf[0, pl.ds(h, 1), rows] = lse[:, h * BLOCK : (h + 1) * BLOCK]
        weights = raised * inverse
        weights_low = weights.astype(BF16)
        score_grad = (weights * (prob - row_dot)).astype(BF16)
        out = dot(vals, weights_low, ((0,), (0,))).astype(BF16)
        query_grad = (dot(keys, score_grad, ((0,), (0,))) * scale).astype(BF16)
        for h in range(GROUP):
            columns = slice(h * BLOCK, (h + 1) * BLOCK)
            obuf[rows, pl.ds(h * HEAD_DIM, HEAD_DIM)] = out[:, columns].T
            st[0, qb, :, pl.ds(h * HEAD_DIM, HEAD_DIM)] = query_grad[:, columns].T
        key_add = dot(score_grad, queries, ((1,), (0,)))
        value_add = dot(weights_low, grads, ((1,), (0,)))
        for b in range(3):
            part = slice(b * BLOCK, (b + 1) * BLOCK)
            add_grad(0, qb + b, key_add[part])
            add_grad(1, qb + b, value_add[part])

    st_swap = [
        remote(st.at[0, t], st.at[1, t], st_s.at[t], st_r.at[t], par) for t in range(BLOCKS)
    ]

    def finish_tokens(t):
        rows = pl.ds((t + REACH_BLOCKS) * BLOCK, BLOCK)
        key_grad = dkv[0, rows, :]
        value_grad = dkv[1, rows, :]
        if t >= 2:
            back = pl.ds((t - 2) * BLOCK, BLOCK)
            key_grad = key_grad + ret[0, back, :]
            value_grad = value_grad + ret[1, back, :]
        st[0, t, :, pl.ds(GROUP * HEAD_DIM, HEAD_DIM)] = (key_grad * scale).astype(BF16)
        st[0, t, :, pl.ds((GROUP + 1) * HEAD_DIM, HEAD_DIM)] = value_grad.astype(BF16)
        st_swap[t].start()

    attend(2)
    attend(3)
    for copy in halo[1]:
        pl.when(has_prev)(copy.wait_recv)
    attend(1)
    finish_tokens(1)
    for copy in halo[0]:
        pl.when(has_prev)(copy.wait_recv)
    attend(0)
    finish_tokens(0)

    back_copy = remote(dkv.at[:, pl.ds(0, 256), :], ret, ret_s, ret_r, prv)
    pl.when(has_prev)(back_copy.start)
    lse_next = remote(lbuf.at[0], lbuf.at[1], lse_s.at[0], lse_r.at[0], nxt)
    lse_prev = remote(lbuf.at[0], lbuf.at[2], lse_s.at[1], lse_r.at[1], prv)
    pl.when(has_next)(lse_next.start)
    pl.when(has_prev)(lse_prev.start)
    out_copy = pltpu.make_async_copy(obuf, o_ref, osem.at[0])
    out_copy.start()

    HALF = BLOCK // 2
    lo, hi = pl.ds(0, HALF), pl.ds(HALF, HALF)
    for r in range(4):
        w_local[r].wait()

    sends = {}
    for t in range(BLOCKS):
        sends[t] = dict(
            h_up=remote(s2.at[t, lo], hp.at[t], rs_s.at[t, 0], rs_r.at[t, 0], up),
            h_dn=remote(s2.at[t, hi], hm.at[t], rs_s.at[t, 1], rs_r.at[t, 1], dn),
            u_up=remote(sp.at[t, hi], rp.at[t, hi], rs_s.at[t, 2], rs_r.at[t, 2], up),
            u_dn=remote(sm.at[t, lo], rm.at[t, lo], rs_s.at[t, 3], rs_r.at[t, 3], dn),
            m_up=remote(sp.at[t, lo], rp.at[t, lo], rs_s.at[t, 4], rs_r.at[t, 4], up),
            m_dn=remote(sm.at[t, hi], rm.at[t, hi], rs_s.at[t, 5], rs_r.at[t, 5], dn),
        )

    def project(t, first_time):
        st_swap[t].wait_recv()

        def part(r):
            if first_time:
                w_swap[r].wait_recv()
            return dot(st[0, t], wown[r], ((1,), (1,))) + dot(st[1, t], wpar[r], ((1,), (1,)))

        s2[t] = part(2).astype(BF16)
        sends[t]["h_up"].start()
        sends[t]["h_dn"].start()
        piece = part(1)
        sp[t, hi, :] = piece[HALF:].astype(BF16)
        sends[t]["u_up"].start()
        mp[t] = piece[:HALF]
        piece = part(3)
        sm[t, lo, :] = piece[:HALF].astype(BF16)
        sends[t]["u_dn"].start()
        mm[t] = piece[HALF:]
        own[t] = part(0)

    def merge(t):
        sends[t]["h_up"].wait_recv()
        sp[t, lo, :] = (mp[t] + hp[t].astype(F32)).astype(BF16)
        sends[t]["m_up"].start()
        sends[t]["h_dn"].wait_recv()
        sm[t, hi, :] = (mm[t] + hm[t].astype(F32)).astype(BF16)
        sends[t]["m_dn"].start()

    gi_copies = []

    def finish(t):
        for name in ("u_up", "u_dn", "m_up", "m_dn"):
            sends[t][name].wait_recv()
        rows = pl.ds(t * BLOCK, BLOCK)
        gibuf[rows, :] = (own[t] + rp[t].astype(F32) + rm[t].astype(F32)).astype(BF16)
        copy = pltpu.make_async_copy(gibuf.at[rows], gi_ref.at[rows], osem.at[1 + t])
        copy.start()
        gi_copies.append(copy)

    project(1, True)
    project(0, False)
    pl.when(has_next)(back_copy.wait_recv)
    finish_tokens(2)
    finish_tokens(3)
    merge(1)
    project(2, False)
    merge(0)
    project(3, False)
    merge(2)

    pl.when(has_prev)(lse_next.wait_recv)
    pl.when(has_next)(lse_prev.wait_recv)
    picked = [jnp.zeros((GROUP, BLOCK), F32) for _ in range(BLOCKS)]
    rank = jnp.int32(0)
    one = jnp.int32(1)
    before, after = jnp.where(has_prev, 1, 0), jnp.where(has_next, 1, 0)
    for source, device, valid in (
        (1, prv["ctx"], before), (0, ctx, one), (2, nxt["ctx"], after),
    ):
        for b in range(BLOCKS):
            hit = jnp.where(plan_ref[device * BLOCKS + b] == ctx, valid, 0)
            piece = lbuf[source, :, pl.ds(b * BLOCK, BLOCK)]
            for s in range(BLOCKS):
                take = jnp.where((hit == 1) & (rank == s), 1.0, 0.0).astype(F32)
                picked[s] = picked[s] + piece * take
            rank = rank + hit
    for s in range(BLOCKS):
        lout[:, pl.ds(s * BLOCK, BLOCK)] = picked[s]
    lse_copy = pltpu.make_async_copy(lout, lse_ref, osem.at[5])
    lse_copy.start()

    merge(3)
    for t in (1, 0, 2, 3):
        finish(t)

    out_copy.wait()
    lse_copy.wait()
    for copy in gi_copies:
        copy.wait()
    for b in (1, 0):
        for copy in halo[b]:
            pl.when(has_next)(copy.wait_send)
    for copy in w_swap:
        copy.wait_send()
    for copy in st_swap:
        copy.wait_send()
    pl.when(has_prev)(back_copy.wait_send)
    pl.when(has_next)(lse_next.wait_send)
    pl.when(has_prev)(lse_prev.wait_send)
    for t in range(BLOCKS):
        for copy in sends[t].values():
            copy.wait_send()


def publish(o_ref, gi_ref, lse_ref, o_out, gi_out, lse_out, sems):
    copies = [pltpu.make_async_copy(lse_ref, lse_out, sems.at[8])]
    for part in range(4):
        rows = pl.ds(part * 128, 128)
        copies.append(pltpu.make_async_copy(gi_ref.at[rows], gi_out.at[rows], sems.at[part]))
        copies.append(pltpu.make_async_copy(o_ref.at[rows], o_out.at[rows], sems.at[4 + part]))
    for copy in copies:
        copy.start()
    for copy in copies:
        copy.wait()


def body(queries, key_states, values, out_grad, weight, lengths, block_plan):
    anywhere = pl.BlockSpec(memory_space=pl.ANY)
    dma = pltpu.SemaphoreType.DMA
    shapes = (
        jax.ShapeDtypeStruct((512, 512), BF16),
        jax.ShapeDtypeStruct((512, 512), BF16),
        jax.ShapeDtypeStruct((GROUP, 512), F32),
    )
    results = pl.pallas_call(
        kernel,
        out_shape=shapes,
        in_specs=[anywhere] * 7,
        out_specs=(anywhere,) * 3,
        scratch_shapes=[
            pltpu.VMEM((768, 128), BF16),
            pltpu.VMEM((768, 128), BF16),
            pltpu.VMEM((512, 512), BF16),
            pltpu.VMEM((512, 512), BF16),
            pltpu.VMEM((4, 512, 768), BF16),
            pltpu.VMEM((4, 512, 768), BF16),
            pltpu.VMEM((2, 768, 128), F32),
            pltpu.VMEM((2, 256, 128), F32),
            pltpu.VMEM((2, 4, 128, 768), BF16),
            pltpu.VMEM((4, 128, 512), BF16),
            pltpu.VMEM((4, 128, 512), BF16),
            pltpu.VMEM((4, 128, 512), BF16),
            pltpu.VMEM((4, 64, 512), BF16),
            pltpu.VMEM((4, 64, 512), BF16),
            pltpu.VMEM((4, 128, 512), BF16),
            pltpu.VMEM((4, 128, 512), BF16),
            pltpu.VMEM((4, 128, 512), F32),
            pltpu.VMEM((4, 64, 512), F32),
            pltpu.VMEM((4, 64, 512), F32),
            pltpu.VMEM((512, 512), BF16),
            pltpu.VMEM((512, 512), BF16),
            pltpu.VMEM((3, GROUP, 512), F32),
            pltpu.VMEM((GROUP, 512), F32),
            pltpu.SMEM(lengths.shape, jnp.int32),
            pltpu.SMEM(block_plan.shape, jnp.int32),
            dma((6,)),
            dma((4,)),
            dma((6,)),
            dma((4,)), dma((4,)),
            dma((4,)), dma((4,)),
            dma((4,)), dma((4,)),
            dma, dma,
            dma((2,)), dma((2,)),
            dma((4, 6)), dma((4, 6)),
        ],
        compiler_params=pltpu.CompilerParams(
            collective_id=0, has_side_effects=True, vmem_limit_bytes=VMEM_LIMIT
        ),
    )(queries, key_states, values, out_grad, weight, lengths, block_plan)
    return pl.pallas_call(
        publish,
        out_shape=shapes,
        in_specs=[anywhere] * 3,
        out_specs=(anywhere,) * 3,
        scratch_shapes=[dma((9,))],
        compiler_params=pltpu.CompilerParams(vmem_limit_bytes=VMEM_LIMIT),
    )(*results)


def solution(mesh):
    in_specs = (
        P("ctx", "tp"),
        P("ctx", "tp"),
        P("ctx", "tp"),
        P("ctx", "tp"),
        P(None, "tp"),
        P(),
        P(),
    )
    out_specs = (P("ctx", "tp"), P("ctx", "tp"), P("tp", "ctx"))
    return jax.shard_map(body, mesh=mesh, in_specs=in_specs, out_specs=out_specs, check_vma=False)
```

```python
import jax
import jax.numpy as jnp
from jax import lax
from jax.experimental import pallas as pl
from jax.experimental.pallas import tpu as pltpu
from jax.sharding import PartitionSpec as P

HEAD_DIM = 128
BLOCK = 128
GROUP = 4
BLOCKS = 4
REACH_BLOCKS = 2
NEG = -1e30
VMEM_LIMIT = 40 * 1024 * 1024
LOG2E = 1.4426950408889634
MESH = pl.DeviceIdType.MESH
F32 = jnp.float32
BF16 = jnp.bfloat16


def dot(a, b, dims):
    return lax.dot_general(a, b, (dims, ((), ())), preferred_element_type=F32)


def remote(src, dst, send, recv, device):
    return pltpu.make_async_remote_copy(
        src_ref=src,
        dst_ref=dst,
        send_sem=send,
        recv_sem=recv,
        device_id=device,
        device_id_type=MESH,
    )


def kernel(
    q_ref, k_ref, v_ref, g_ref, w_ref, len_hbm, plan_hbm,
    o_ref, gi_ref, lse_ref,
    kbuf, vbuf, qbuf, gbuf, wown, wpar, dkv, ret, st,
    s2, sp, sm, hp, hm, rp, rm, own, mp, mm,
    obuf, gibuf, lbuf, lout, len_ref, plan_ref,
    lsem, wsem, osem,
    halo_s, halo_r, w_s, w_r, st_s, st_r, ret_s, ret_r, lse_s, lse_r, rs_s, rs_r,
):
    n_ctx = lax.axis_size("ctx")
    n_tp = lax.axis_size("tp")
    n_y = n_tp // 2
    ctx = lax.axis_index("ctx")
    tp = lax.axis_index("tp")
    y = tp // 2
    core = tp - 2 * y
    nxt = {"ctx": lax.rem(ctx + 1, n_ctx)}
    prv = {"ctx": lax.rem(ctx + n_ctx - 1, n_ctx)}
    par = {"tp": tp + 1 - 2 * core}
    up = {"tp": lax.rem(tp + 2, n_tp)}
    dn = {"tp": lax.rem(tp + n_tp - 2, n_tp)}

    has_next = ctx < n_ctx - 1
    has_prev = ctx > 0

    def greet(device):
        pl.semaphore_signal(barrier, inc=1, device_id=device, device_id_type=MESH)

    barrier = pltpu.get_barrier_semaphore()
    pl.when(has_next)(lambda: greet(nxt))
    pl.when(has_prev)(lambda: greet(prv))
    for device in (par, up, dn):
        greet(device)
    len_copy = pltpu.make_async_copy(len_hbm, len_ref, lsem.at[4])
    plan_copy = pltpu.make_async_copy(plan_hbm, plan_ref, lsem.at[5])
    len_copy.start()
    plan_copy.start()

    locals_ = [
        pltpu.make_async_copy(k_ref, kbuf.at[pl.ds(256, 512)], lsem.at[0]),
        pltpu.make_async_copy(q_ref, qbuf, lsem.at[1]),
        pltpu.make_async_copy(v_ref, vbuf.at[pl.ds(256, 512)], lsem.at[2]),
        pltpu.make_async_copy(g_ref, gbuf, lsem.at[3]),
    ]
    for copy in locals_:
        copy.start()

    def w_rows(r, c):
        return pl.ds(pl.multiple_of((2 * lax.rem(y + r, n_y) + c) * 512, 512), 512)

    w_local = [
        pltpu.make_async_copy(w_ref.at[w_rows(r, core)], wown.at[r], wsem.at[r])
        for r in range(4)
    ]
    for r in (2, 1, 3, 0):
        w_local[r].start()

    def no_halo():
        kbuf[pl.ds(0, 256), :] = jnp.zeros((256, 128), BF16)
        vbuf[pl.ds(0, 256), :] = jnp.zeros((256, 128), BF16)
        lbuf[1] = jnp.zeros((GROUP, 512), F32)

    def no_return():
        ret[...] = jnp.zeros((2, 256, 128), F32)
        lbuf[2] = jnp.zeros((GROUP, 512), F32)

    pl.when(jnp.logical_not(has_prev))(no_halo)
    pl.when(jnp.logical_not(has_next))(no_return)

    first = ctx * BLOCKS

    def scan_lengths(i, carry):
        total = carry[0] + len_ref[i]
        return (total,) + tuple(
            carry[1 + b] + jnp.where(total == (first + b - 1) * BLOCK, 1, 0)
            for b in range(5)
        )

    start = jnp.int32(0)
    edge = jnp.where(ctx == 0, 1, 0).astype(jnp.int32)
    len_copy.wait()
    plan_copy.wait()
    found = lax.fori_loop(
        0, len_ref.shape[0], scan_lengths, (start, start, edge, start, start, start)
    )[1:]

    pl.semaphore_wait(
        barrier, 3 + jnp.where(has_next, 1, 0) + jnp.where(has_prev, 1, 0)
    )

    halo = {}
    slot = 0
    for b in (1, 0):
        for src, dst in ((k_ref, kbuf), (v_ref, vbuf)):
            copy = remote(
                src.at[pl.ds(256 + b * BLOCK, BLOCK)],
                dst.at[pl.ds(b * BLOCK, BLOCK)],
                halo_s.at[slot], halo_r.at[slot], nxt,
            )
            pl.when(has_next)(copy.start)
            halo.setdefault(b, []).append(copy)
            slot += 1
    w_swap = [
        remote(w_ref.at[w_rows(r, 1 - core)], wpar.at[r], w_s.at[r], w_r.at[r], par)
        for r in range(4)
    ]
    for r in (2, 1, 3, 0):
        w_swap[r].start()

    for copy in locals_:
        copy.wait()

    scale = HEAD_DIM ** -0.5
    causal = lax.broadcasted_iota(jnp.int32, (BLOCK, BLOCK), 0) <= lax.broadcasted_iota(
        jnp.int32, (BLOCK, BLOCK), 1
    )
    causal_bias = jnp.where(causal, 0.0, NEG).astype(F32)
    causal_bias = jnp.concatenate([causal_bias] * GROUP, axis=1)
    written = set()

    def add_grad(which, index, value):
        rows = pl.ds(index * BLOCK, BLOCK)
        if (which, index) in written:
            dkv[which, rows, :] += value
        else:
            written.add((which, index))
            dkv[which, rows, :] = value

    def heads_in_rows(ref, qb):
        rows = pl.ds(qb * BLOCK, BLOCK)
        return jnp.concatenate(
            [ref[rows, pl.ds(h * HEAD_DIM, HEAD_DIM)] for h in range(GROUP)], axis=0
        )

    def attend(qb):
        rows = pl.ds(qb * BLOCK, BLOCK)
        keys = kbuf[pl.ds(qb * BLOCK, 3 * BLOCK), :]
        vals = vbuf[pl.ds(qb * BLOCK, 3 * BLOCK), :]
        queries = heads_in_rows(qbuf, qb)
        grads = heads_in_rows(gbuf, qb)
        near = jnp.where(found[qb + 1] > 0, NEG, 0.0).astype(F32)
        far = jnp.where(found[qb + 1] + found[qb] > 0, NEG, 0.0).astype(F32)
        scores = dot(keys, queries, ((1,), (1,)))
        prob = dot(vals, grads, ((1,), (1,)))
        scores = jnp.concatenate(
            [
                scores[:BLOCK] + far,
                scores[BLOCK : 2 * BLOCK] + near,
                scores[2 * BLOCK :] + causal_bias,
            ],
            axis=0,
        )
        top = jnp.max(scores, axis=0, keepdims=True)
        raised = jnp.exp2((scores - top) * (scale * LOG2E))
        total = jnp.sum(raised, axis=0, keepdims=True)
        mixed = jnp.sum(raised * prob, axis=0, keepdims=True)
        inverse = 1.0 / total
        row_dot = mixed * inverse
        lse = top * scale + jnp.log(total)
        for h in range(GROUP):
            lbuf[0, pl.ds(h, 1), rows] = lse[:, h * BLOCK : (h + 1) * BLOCK]
        weights = raised * inverse
        weights_low = weights.astype(BF16)
        score_grad = (weights * (prob - row_dot)).astype(BF16)
        out = dot(vals, weights_low, ((0,), (0,))).astype(BF16)
        query_grad = (dot(keys, score_grad, ((0,), (0,))) * scale).astype(BF16)
        for h in range(GROUP):
            columns = slice(h * BLOCK, (h + 1) * BLOCK)
            obuf[rows, pl.ds(h * HEAD_DIM, HEAD_DIM)] = out[:, columns].T
            st[0, qb, :, pl.ds(h * HEAD_DIM, HEAD_DIM)] = query_grad[:, columns].T
        key_add = dot(score_grad, queries, ((1,), (0,)))
        value_add = dot(weights_low, grads, ((1,), (0,)))
        for b in range(3):
            part = slice(b * BLOCK, (b + 1) * BLOCK)
            add_grad(0, qb + b, key_add[part])
            add_grad(1, qb + b, value_add[part])

    st_swap = [
        remote(st.at[0, t], st.at[1, t], st_s.at[t], st_r.at[t], par) for t in range(BLOCKS)
    ]

    def finish_tokens(t):
        rows = pl.ds((t + REACH_BLOCKS) * BLOCK, BLOCK)
        key_grad = dkv[0, rows, :]
        value_grad = dkv[1, rows, :]
        if t >= 2:
            back = pl.ds((t - 2) * BLOCK, BLOCK)
            key_grad = key_grad + ret[0, back, :]
            value_grad = value_grad + ret[1, back, :]
        st[0, t, :, pl.ds(GROUP * HEAD_DIM, HEAD_DIM)] = (key_grad * scale).astype(BF16)
        st[0, t, :, pl.ds((GROUP + 1) * HEAD_DIM, HEAD_DIM)] = value_grad.astype(BF16)
        st_swap[t].start()

    attend(2)
    attend(3)
    for copy in halo[1]:
        pl.when(has_prev)(copy.wait_recv)
    attend(1)
    finish_tokens(1)
    for copy in halo[0]:
        pl.when(has_prev)(copy.wait_recv)
    attend(0)
    finish_tokens(0)

    back_copy = remote(dkv.at[:, pl.ds(0, 256), :], ret, ret_s, ret_r, prv)
    pl.when(has_prev)(back_copy.start)
    lse_next = remote(lbuf.at[0], lbuf.at[1], lse_s.at[0], lse_r.at[0], nxt)
    lse_prev = remote(lbuf.at[0], lbuf.at[2], lse_s.at[1], lse_r.at[1], prv)
    pl.when(has_next)(lse_next.start)
    pl.when(has_prev)(lse_prev.start)
    out_copy = pltpu.make_async_copy(obuf, o_ref, osem.at[0])
    out_copy.start()

    HALF = BLOCK // 2
    lo, hi = pl.ds(0, HALF), pl.ds(HALF, HALF)
    for r in range(4):
        w_local[r].wait()

    sends = {}
    for t in range(BLOCKS):
        sends[t] = dict(
            h_up=remote(s2.at[t, lo], hp.at[t], rs_s.at[t, 0], rs_r.at[t, 0], up),
            h_dn=remote(s2.at[t, hi], hm.at[t], rs_s.at[t, 1], rs_r.at[t, 1], dn),
            u_up=remote(sp.at[t, hi], rp.at[t, hi], rs_s.at[t, 2], rs_r.at[t, 2], up),
            u_dn=remote(sm.at[t, lo], rm.at[t, lo], rs_s.at[t, 3], rs_r.at[t, 3], dn),
            m_up=remote(sp.at[t, lo], rp.at[t, lo], rs_s.at[t, 4], rs_r.at[t, 4], up),
            m_dn=remote(sm.at[t, hi], rm.at[t, hi], rs_s.at[t, 5], rs_r.at[t, 5], dn),
        )

    def project(t, first_time):
        st_swap[t].wait_recv()

        def part(r):
            if first_time:
                w_swap[r].wait_recv()
            return dot(st[0, t], wown[r], ((1,), (1,))) + dot(st[1, t], wpar[r], ((1,), (1,)))

        s2[t] = part(2).astype(BF16)
        sends[t]["h_up"].start()
        sends[t]["h_dn"].start()
        piece = part(1)
        sp[t, hi, :] = piece[HALF:].astype(BF16)
        sends[t]["u_up"].start()
        mp[t] = piece[:HALF]
        piece = part(3)
        sm[t, lo, :] = piece[:HALF].astype(BF16)
        sends[t]["u_dn"].start()
        mm[t] = piece[HALF:]
        own[t] = part(0)

    def merge(t):
        sends[t]["h_up"].wait_recv()
        sp[t, lo, :] = (mp[t] + hp[t].astype(F32)).astype(BF16)
        sends[t]["m_up"].start()
        sends[t]["h_dn"].wait_recv()
        sm[t, hi, :] = (mm[t] + hm[t].astype(F32)).astype(BF16)
        sends[t]["m_dn"].start()

    gi_copies = []

    def finish(t):
        for name in ("u_up", "u_dn", "m_up", "m_dn"):
            sends[t][name].wait_recv()
        rows = pl.ds(t * BLOCK, BLOCK)
        gibuf[rows, :] = (own[t] + rp[t].astype(F32) + rm[t].astype(F32)).astype(BF16)
        copy = pltpu.make_async_copy(gibuf.at[rows], gi_ref.at[rows], osem.at[1 + t])
        copy.start()
        gi_copies.append(copy)

    project(1, True)
    project(0, False)
    pl.when(has_next)(back_copy.wait_recv)
    finish_tokens(2)
    finish_tokens(3)
    merge(1)
    project(2, False)
    merge(0)
    project(3, False)
    merge(2)

    pl.when(has_prev)(lse_next.wait_recv)
    pl.when(has_next)(lse_prev.wait_recv)
    picked = [jnp.zeros((GROUP, BLOCK), F32) for _ in range(BLOCKS)]
    rank = jnp.int32(0)
    one = jnp.int32(1)
    before, after = jnp.where(has_prev, 1, 0), jnp.where(has_next, 1, 0)
    for source, device, valid in (
        (1, prv["ctx"], before), (0, ctx, one), (2, nxt["ctx"], after),
    ):
        for b in range(BLOCKS):
            hit = jnp.where(plan_ref[device * BLOCKS + b] == ctx, valid, 0)
            piece = lbuf[source, :, pl.ds(b * BLOCK, BLOCK)]
            for s in range(BLOCKS):
                take = jnp.where((hit == 1) & (rank == s), 1.0, 0.0).astype(F32)
                picked[s] = picked[s] + piece * take
            rank = rank + hit
    for s in range(BLOCKS):
        lout[:, pl.ds(s * BLOCK, BLOCK)] = picked[s]
    lse_copy = pltpu.make_async_copy(lout, lse_ref, osem.at[5])
    lse_copy.start()

    merge(3)
    for t in (1, 0, 2, 3):
        finish(t)

    out_copy.wait()
    lse_copy.wait()
    for copy in gi_copies:
        copy.wait()
    for b in (1, 0):
        for copy in halo[b]:
            pl.when(has_next)(copy.wait_send)
    for copy in w_swap:
        copy.wait_send()
    for copy in st_swap:
        copy.wait_send()
    pl.when(has_prev)(back_copy.wait_send)
    pl.when(has_next)(lse_next.wait_send)
    pl.when(has_prev)(lse_prev.wait_send)
    for t in range(BLOCKS):
        for copy in sends[t].values():
            copy.wait_send()


def publish(o_ref, gi_ref, lse_ref, o_out, gi_out, lse_out, sems):
    copies = [pltpu.make_async_copy(lse_ref, lse_out, sems.at[8])]
    for part in range(4):
        rows = pl.ds(part * 128, 128)
        copies.append(pltpu.make_async_copy(gi_ref.at[rows], gi_out.at[rows], sems.at[part]))
        copies.append(pltpu.make_async_copy(o_ref.at[rows], o_out.at[rows], sems.at[4 + part]))
    for copy in copies:
        copy.start()
    for copy in copies:
        copy.wait()


def body(queries, key_states, values, out_grad, weight, lengths, block_plan):
    anywhere = pl.BlockSpec(memory_space=pl.ANY)
    dma = pltpu.SemaphoreType.DMA
    shapes = (
        jax.ShapeDtypeStruct((512, 512), BF16),
        jax.ShapeDtypeStruct((512, 512), BF16),
        jax.ShapeDtypeStruct((GROUP, 512), F32),
    )
    operands = [
        pltpu.with_memory_space_constraint(operand, pltpu.HBM)
        for operand in (queries, key_states, values, out_grad, weight, lengths, block_plan)
    ]
    results = pl.pallas_call(
        kernel,
        out_shape=shapes,
        in_specs=[anywhere] * 7,
        out_specs=(anywhere,) * 3,
        scratch_shapes=[
            pltpu.VMEM((768, 128), BF16),
            pltpu.VMEM((768, 128), BF16),
            pltpu.VMEM((512, 512), BF16),
            pltpu.VMEM((512, 512), BF16),
            pltpu.VMEM((4, 512, 768), BF16),
            pltpu.VMEM((4, 512, 768), BF16),
            pltpu.VMEM((2, 768, 128), F32),
            pltpu.VMEM((2, 256, 128), F32),
            pltpu.VMEM((2, 4, 128, 768), BF16),
            pltpu.VMEM((4, 128, 512), BF16),
            pltpu.VMEM((4, 128, 512), BF16),
            pltpu.VMEM((4, 128, 512), BF16),
            pltpu.VMEM((4, 64, 512), BF16),
            pltpu.VMEM((4, 64, 512), BF16),
            pltpu.VMEM((4, 128, 512), BF16),
            pltpu.VMEM((4, 128, 512), BF16),
            pltpu.VMEM((4, 128, 512), F32),
            pltpu.VMEM((4, 64, 512), F32),
            pltpu.VMEM((4, 64, 512), F32),
            pltpu.VMEM((512, 512), BF16),
            pltpu.VMEM((512, 512), BF16),
            pltpu.VMEM((3, GROUP, 512), F32),
            pltpu.VMEM((GROUP, 512), F32),
            pltpu.SMEM(lengths.shape, jnp.int32),
            pltpu.SMEM(block_plan.shape, jnp.int32),
            dma((6,)),
            dma((4,)),
            dma((6,)),
            dma((4,)), dma((4,)),
            dma((4,)), dma((4,)),
            dma((4,)), dma((4,)),
            dma, dma,
            dma((2,)), dma((2,)),
            dma((4, 6)), dma((4, 6)),
        ],
        compiler_params=pltpu.CompilerParams(
            collective_id=0, has_side_effects=True, vmem_limit_bytes=VMEM_LIMIT
        ),
    )(*operands)
    return pl.pallas_call(
        publish,
        out_shape=shapes,
        in_specs=[anywhere] * 3,
        out_specs=(anywhere,) * 3,
        scratch_shapes=[dma((9,))],
        compiler_params=pltpu.CompilerParams(vmem_limit_bytes=VMEM_LIMIT),
    )(*results)


def solution(mesh):
    in_specs = (
        P("ctx", "tp"),
        P("ctx", "tp"),
        P("ctx", "tp"),
        P("ctx", "tp"),
        P(None, "tp"),
        P(),
        P(),
    )
    out_specs = (P("ctx", "tp"), P("ctx", "tp"), P("tp", "ctx"))
    return jax.shard_map(body, mesh=mesh, in_specs=in_specs, out_specs=out_specs, check_vma=False)
```

```python
import jax
import jax.numpy as jnp
from jax import lax
from jax.experimental import pallas as pl
from jax.experimental.pallas import tpu as pltpu
from jax.sharding import PartitionSpec as P

HEAD_DIM = 128
BLOCK = 128
GROUP = 4
BLOCKS = 4
REACH_BLOCKS = 2
NEG = -1e30
VMEM_LIMIT = 40 * 1024 * 1024
LOG2E = 1.4426950408889634
MESH = pl.DeviceIdType.MESH
F32 = jnp.float32
BF16 = jnp.bfloat16


def dot(a, b, dims):
    return lax.dot_general(a, b, (dims, ((), ())), preferred_element_type=F32)


def remote(src, dst, send, recv, device):
    return pltpu.make_async_remote_copy(
        src_ref=src,
        dst_ref=dst,
        send_sem=send,
        recv_sem=recv,
        device_id=device,
        device_id_type=MESH,
    )


def kernel(
    q_ref, k_ref, v_ref, g_ref, w_ref, len_hbm, plan_hbm,
    o_ref, gi_ref, lse_ref,
    kbuf, vbuf, qbuf, gbuf, wown, wpar, dkv, leave, ret, st,
    s2, sp, sm, hp, hm, rp, rm, own, mp, mm,
    obuf, gibuf, lbuf, lout, len_ref, plan_ref,
    lsem, wsem, osem,
    halo_s, halo_r, w_s, w_r, st_s, st_r, ret_s, ret_r, lse_s, lse_r, rs_s, rs_r,
):
    n_ctx = lax.axis_size("ctx")
    n_tp = lax.axis_size("tp")
    n_y = n_tp // 2
    ctx = lax.axis_index("ctx")
    tp = lax.axis_index("tp")
    y = tp // 2
    core = tp - 2 * y
    nxt = {"ctx": lax.rem(ctx + 1, n_ctx)}
    prv = {"ctx": lax.rem(ctx + n_ctx - 1, n_ctx)}
    par = {"tp": tp + 1 - 2 * core}
    up = {"tp": lax.rem(tp + 2, n_tp)}
    dn = {"tp": lax.rem(tp + n_tp - 2, n_tp)}

    has_next = ctx < n_ctx - 1
    has_prev = ctx > 0

    def greet(device):
        pl.semaphore_signal(barrier, inc=1, device_id=device, device_id_type=MESH)

    barrier = pltpu.get_barrier_semaphore()
    pl.when(has_next)(lambda: greet(nxt))
    pl.when(has_prev)(lambda: greet(prv))
    for device in (par, up, dn):
        greet(device)
    len_copy = pltpu.make_async_copy(len_hbm, len_ref, lsem.at[4])
    plan_copy = pltpu.make_async_copy(plan_hbm, plan_ref, lsem.at[5])
    len_copy.start()
    plan_copy.start()

    locals_ = [
        pltpu.make_async_copy(k_ref, kbuf.at[pl.ds(256, 512)], lsem.at[0]),
        pltpu.make_async_copy(q_ref, qbuf, lsem.at[1]),
        pltpu.make_async_copy(v_ref, vbuf.at[pl.ds(256, 512)], lsem.at[2]),
        pltpu.make_async_copy(g_ref, gbuf, lsem.at[3]),
    ]
    for copy in locals_:
        copy.start()

    def w_rows(r, c):
        return pl.ds(pl.multiple_of((2 * lax.rem(y + r, n_y) + c) * 512, 512), 512)

    w_local = [
        pltpu.make_async_copy(w_ref.at[w_rows(r, core)], wown.at[r], wsem.at[r])
        for r in range(4)
    ]
    for r in (2, 1, 3, 0):
        w_local[r].start()

    def no_halo():
        kbuf[pl.ds(0, 256), :] = jnp.zeros((256, 128), BF16)
        vbuf[pl.ds(0, 256), :] = jnp.zeros((256, 128), BF16)
        lbuf[1] = jnp.zeros((GROUP, 512), F32)

    def no_return():
        ret[...] = jnp.zeros((2, 2, 128, 128), BF16)
        lbuf[2] = jnp.zeros((GROUP, 512), F32)

    pl.when(jnp.logical_not(has_prev))(no_halo)
    pl.when(jnp.logical_not(has_next))(no_return)

    first = ctx * BLOCKS

    def scan_lengths(i, carry):
        total = carry[0] + len_ref[i]
        return (total,) + tuple(
            carry[1 + b] + jnp.where(total == (first + b - 1) * BLOCK, 1, 0)
            for b in range(5)
        )

    start = jnp.int32(0)
    edge = jnp.where(ctx == 0, 1, 0).astype(jnp.int32)
    len_copy.wait()
    plan_copy.wait()
    found = lax.fori_loop(
        0, len_ref.shape[0], scan_lengths, (start, start, edge, start, start, start)
    )[1:]

    locals_[0].wait()
    locals_[2].wait()
    pl.semaphore_wait(
        barrier, 3 + jnp.where(has_next, 1, 0) + jnp.where(has_prev, 1, 0)
    )

    halo = {}
    slot = 0
    for b in (1, 0):
        for buf in (kbuf, vbuf):
            copy = remote(
                buf.at[pl.ds(512 + b * BLOCK, BLOCK)],
                buf.at[pl.ds(b * BLOCK, BLOCK)],
                halo_s.at[slot], halo_r.at[slot], nxt,
            )
            pl.when(has_next)(copy.start)
            halo.setdefault(b, []).append(copy)
            slot += 1
    w_swap = [
        remote(w_ref.at[w_rows(r, 1 - core)], wpar.at[r], w_s.at[r], w_r.at[r], par)
        for r in range(4)
    ]
    for r in (2, 1, 3, 0):
        w_swap[r].start()

    locals_[1].wait()
    locals_[3].wait()

    scale = HEAD_DIM ** -0.5
    causal = lax.broadcasted_iota(jnp.int32, (BLOCK, BLOCK), 0) <= lax.broadcasted_iota(
        jnp.int32, (BLOCK, BLOCK), 1
    )
    causal_bias = jnp.where(causal, 0.0, NEG).astype(F32)
    causal_bias = jnp.concatenate([causal_bias] * GROUP, axis=1)
    written = set()

    def add_grad(which, index, value):
        rows = pl.ds(index * BLOCK, BLOCK)
        if (which, index) in written:
            dkv[which, rows, :] += value
        else:
            written.add((which, index))
            dkv[which, rows, :] = value

    def heads_in_rows(ref, qb):
        rows = pl.ds(qb * BLOCK, BLOCK)
        return jnp.concatenate(
            [ref[rows, pl.ds(h * HEAD_DIM, HEAD_DIM)] for h in range(GROUP)], axis=0
        )

    def attend(qb):
        rows = pl.ds(qb * BLOCK, BLOCK)
        keys = kbuf[pl.ds(qb * BLOCK, 3 * BLOCK), :]
        vals = vbuf[pl.ds(qb * BLOCK, 3 * BLOCK), :]
        queries = heads_in_rows(qbuf, qb)
        grads = heads_in_rows(gbuf, qb)
        near = jnp.where(found[qb + 1] > 0, NEG, 0.0).astype(F32)
        far = jnp.where(found[qb + 1] + found[qb] > 0, NEG, 0.0).astype(F32)
        scores = dot(keys, queries, ((1,), (1,)))
        prob = dot(vals, grads, ((1,), (1,)))
        scores = jnp.concatenate(
            [
                scores[:BLOCK] + far,
                scores[BLOCK : 2 * BLOCK] + near,
                scores[2 * BLOCK :] + causal_bias,
            ],
            axis=0,
        )
        top = jnp.max(scores, axis=0, keepdims=True)
        raised = jnp.exp2((scores - top) * (scale * LOG2E))
        total = jnp.sum(raised, axis=0, keepdims=True)
        mixed = jnp.sum(raised * prob, axis=0, keepdims=True)
        inverse = 1.0 / total
        row_dot = mixed * inverse
        lse = top * scale + jnp.log(total)
        for h in range(GROUP):
            lbuf[0, pl.ds(h, 1), rows] = lse[:, h * BLOCK : (h + 1) * BLOCK]
        weights = raised * inverse
        weights_low = weights.astype(BF16)
        score_grad = (weights * (prob - row_dot)).astype(BF16)
        out = dot(vals, weights_low, ((0,), (0,))).astype(BF16)
        query_grad = (dot(keys, score_grad, ((0,), (0,))) * scale).astype(BF16)
        for h in range(GROUP):
            columns = slice(h * BLOCK, (h + 1) * BLOCK)
            o_ref[rows, pl.ds(h * HEAD_DIM, HEAD_DIM)] = out[:, columns].T
            st[0, qb, :, pl.ds(h * HEAD_DIM, HEAD_DIM)] = query_grad[:, columns].T
        key_add = dot(score_grad, queries, ((1,), (0,)))
        value_add = dot(weights_low, grads, ((1,), (0,)))
        for b in range(3):
            part = slice(b * BLOCK, (b + 1) * BLOCK)
            add_grad(0, qb + b, key_add[part])
            add_grad(1, qb + b, value_add[part])

    st_swap = [
        remote(st.at[0, t], st.at[1, t], st_s.at[t], st_r.at[t], par) for t in range(BLOCKS)
    ]

    back_copies = [
        remote(leave.at[b], ret.at[b], ret_s.at[b], ret_r.at[b], prv)
        for b in range(REACH_BLOCKS)
    ]

    def finish_tokens(t):
        rows = pl.ds((t + REACH_BLOCKS) * BLOCK, BLOCK)
        key_grad = dkv[0, rows, :]
        value_grad = dkv[1, rows, :]
        if t >= 2:
            pl.when(has_next)(back_copies[t - 2].wait_recv)
            key_grad = key_grad + ret[t - 2, 0].astype(F32)
            value_grad = value_grad + ret[t - 2, 1].astype(F32)
        st[0, t, :, pl.ds(GROUP * HEAD_DIM, HEAD_DIM)] = (key_grad * scale).astype(BF16)
        st[0, t, :, pl.ds((GROUP + 1) * HEAD_DIM, HEAD_DIM)] = value_grad.astype(BF16)
        st_swap[t].start()

    attend(2)
    attend(3)
    for copy in halo[1]:
        pl.when(has_prev)(copy.wait_recv)
    attend(1)
    finish_tokens(1)
    for copy in halo[0]:
        pl.when(has_prev)(copy.wait_recv)
    attend(0)
    finish_tokens(0)

    for b in range(REACH_BLOCKS):
        for which in range(2):
            leave[b, which] = dkv[which, pl.ds(b * BLOCK, BLOCK), :].astype(BF16)
        pl.when(has_prev)(back_copies[b].start)
    lse_next = remote(lbuf.at[0], lbuf.at[1], lse_s.at[0], lse_r.at[0], nxt)
    lse_prev = remote(lbuf.at[0], lbuf.at[2], lse_s.at[1], lse_r.at[1], prv)
    pl.when(has_next)(lse_next.start)
    pl.when(has_prev)(lse_prev.start)

    HALF = BLOCK // 2
    lo, hi = pl.ds(0, HALF), pl.ds(HALF, HALF)
    for r in range(4):
        w_local[r].wait()

    sends = {}
    for t in range(BLOCKS):
        sends[t] = dict(
            h_up=remote(s2.at[t, lo], hp.at[t], rs_s.at[t, 0], rs_r.at[t, 0], up),
            h_dn=remote(s2.at[t, hi], hm.at[t], rs_s.at[t, 1], rs_r.at[t, 1], dn),
            u_up=remote(sp.at[t, hi], rp.at[t, hi], rs_s.at[t, 2], rs_r.at[t, 2], up),
            u_dn=remote(sm.at[t, lo], rm.at[t, lo], rs_s.at[t, 3], rs_r.at[t, 3], dn),
            m_up=remote(sp.at[t, lo], rp.at[t, lo], rs_s.at[t, 4], rs_r.at[t, 4], up),
            m_dn=remote(sm.at[t, hi], rm.at[t, hi], rs_s.at[t, 5], rs_r.at[t, 5], dn),
        )

    def project(t, first_time):
        st_swap[t].wait_recv()

        def part(r):
            if first_time:
                w_swap[r].wait_recv()
            return dot(st[0, t], wown[r], ((1,), (1,))) + dot(st[1, t], wpar[r], ((1,), (1,)))

        s2[t] = part(2).astype(BF16)
        sends[t]["h_up"].start()
        sends[t]["h_dn"].start()
        piece = part(1)
        sp[t, hi, :] = piece[HALF:].astype(BF16)
        sends[t]["u_up"].start()
        mp[t] = piece[:HALF]
        piece = part(3)
        sm[t, lo, :] = piece[:HALF].astype(BF16)
        sends[t]["u_dn"].start()
        mm[t] = piece[HALF:]
        own[t] = part(0)

    def merge(t):
        sends[t]["h_up"].wait_recv()
        sp[t, lo, :] = (mp[t] + hp[t].astype(F32)).astype(BF16)
        sends[t]["m_up"].start()
        sends[t]["h_dn"].wait_recv()
        sm[t, hi, :] = (mm[t] + hm[t].astype(F32)).astype(BF16)
        sends[t]["m_dn"].start()

    def finish(t):
        for name in ("u_up", "u_dn", "m_up", "m_dn"):
            sends[t][name].wait_recv()
        rows = pl.ds(t * BLOCK, BLOCK)
        gi_ref[rows, :] = (own[t] + rp[t].astype(F32) + rm[t].astype(F32)).astype(BF16)

    project(1, True)
    project(0, False)
    merge(1)
    finish_tokens(2)
    finish_tokens(3)
    merge(0)
    project(2, False)
    project(3, False)
    merge(2)

    pl.when(has_prev)(lse_next.wait_recv)
    pl.when(has_next)(lse_prev.wait_recv)
    picked = [jnp.zeros((GROUP, BLOCK), F32) for _ in range(BLOCKS)]
    rank = jnp.int32(0)
    one = jnp.int32(1)
    before, after = jnp.where(has_prev, 1, 0), jnp.where(has_next, 1, 0)
    for source, device, valid in (
        (1, prv["ctx"], before), (0, ctx, one), (2, nxt["ctx"], after),
    ):
        for b in range(BLOCKS):
            hit = jnp.where(plan_ref[device * BLOCKS + b] == ctx, valid, 0)
            piece = lbuf[source, :, pl.ds(b * BLOCK, BLOCK)]
            for s in range(BLOCKS):
                take = jnp.where((hit == 1) & (rank == s), 1.0, 0.0).astype(F32)
                picked[s] = picked[s] + piece * take
            rank = rank + hit
    for s in range(BLOCKS):
        lse_ref[:, pl.ds(s * BLOCK, BLOCK)] = picked[s]

    finish(1)
    finish(0)
    merge(3)
    finish(2)
    finish(3)

    for b in (1, 0):
        for copy in halo[b]:
            pl.when(has_next)(copy.wait_send)
    for copy in w_swap:
        copy.wait_send()
    for copy in st_swap:
        copy.wait_send()
    for copy in back_copies:
        pl.when(has_prev)(copy.wait_send)
    pl.when(has_next)(lse_next.wait_send)
    pl.when(has_prev)(lse_prev.wait_send)
    for t in range(BLOCKS):
        for copy in sends[t].values():
            copy.wait_send()


def publish(o_ref, gi_ref, lse_ref, o_out, gi_out, lse_out, sems):
    copies = [pltpu.make_async_copy(lse_ref, lse_out, sems.at[8])]
    for part in range(4):
        rows = pl.ds(part * 128, 128)
        copies.append(pltpu.make_async_copy(gi_ref.at[rows], gi_out.at[rows], sems.at[part]))
        copies.append(pltpu.make_async_copy(o_ref.at[rows], o_out.at[rows], sems.at[4 + part]))
    for copy in copies:
        copy.start()
    for copy in copies:
        copy.wait()


def body(queries, key_states, values, out_grad, weight, lengths, block_plan):
    anywhere = pl.BlockSpec(memory_space=pl.ANY)
    dma = pltpu.SemaphoreType.DMA
    shapes = (
        jax.ShapeDtypeStruct((512, 512), BF16),
        jax.ShapeDtypeStruct((512, 512), BF16),
        jax.ShapeDtypeStruct((GROUP, 512), F32),
    )
    operands = [
        pltpu.with_memory_space_constraint(operand, pltpu.HBM)
        for operand in (queries, key_states, values, out_grad, weight, lengths, block_plan)
    ]
    results = pl.pallas_call(
        kernel,
        out_shape=shapes,
        in_specs=[anywhere] * 7,
        out_specs=(pl.BlockSpec(memory_space=pltpu.VMEM),) * 3,
        scratch_shapes=[
            pltpu.VMEM((768, 128), BF16),
            pltpu.VMEM((768, 128), BF16),
            pltpu.VMEM((512, 512), BF16),
            pltpu.VMEM((512, 512), BF16),
            pltpu.VMEM((4, 512, 768), BF16),
            pltpu.VMEM((4, 512, 768), BF16),
            pltpu.VMEM((2, 768, 128), F32),
            pltpu.VMEM((2, 2, 128, 128), BF16),
            pltpu.VMEM((2, 2, 128, 128), BF16),
            pltpu.VMEM((2, 4, 128, 768), BF16),
            pltpu.VMEM((4, 128, 512), BF16),
            pltpu.VMEM((4, 128, 512), BF16),
            pltpu.VMEM((4, 128, 512), BF16),
            pltpu.VMEM((4, 64, 512), BF16),
            pltpu.VMEM((4, 64, 512), BF16),
            pltpu.VMEM((4, 128, 512), BF16),
            pltpu.VMEM((4, 128, 512), BF16),
            pltpu.VMEM((4, 128, 512), F32),
            pltpu.VMEM((4, 64, 512), F32),
            pltpu.VMEM((4, 64, 512), F32),
            pltpu.VMEM((512, 512), BF16),
            pltpu.VMEM((512, 512), BF16),
            pltpu.VMEM((3, GROUP, 512), F32),
            pltpu.VMEM((GROUP, 512), F32),
            pltpu.SMEM(lengths.shape, jnp.int32),
            pltpu.SMEM(block_plan.shape, jnp.int32),
            dma((6,)),
            dma((4,)),
            dma((6,)),
            dma((4,)), dma((4,)),
            dma((4,)), dma((4,)),
            dma((4,)), dma((4,)),
            dma((2,)), dma((2,)),
            dma((2,)), dma((2,)),
            dma((4, 6)), dma((4, 6)),
        ],
        compiler_params=pltpu.CompilerParams(
            collective_id=0, has_side_effects=True, vmem_limit_bytes=VMEM_LIMIT
        ),
    )(*operands)
    return pl.pallas_call(
        publish,
        out_shape=shapes,
        in_specs=[anywhere] * 3,
        out_specs=(anywhere,) * 3,
        scratch_shapes=[dma((9,))],
        compiler_params=pltpu.CompilerParams(vmem_limit_bytes=VMEM_LIMIT),
    )(*results)


def solution(mesh):
    in_specs = (
        P("ctx", "tp"),
        P("ctx", "tp"),
        P("ctx", "tp"),
        P("ctx", "tp"),
        P(None, "tp"),
        P(),
        P(),
    )
    out_specs = (P("ctx", "tp"), P("ctx", "tp"), P("tp", "ctx"))
    return jax.shard_map(body, mesh=mesh, in_specs=in_specs, out_specs=out_specs, check_vma=False)
```

```python
import jax
import jax.numpy as jnp
from jax import lax
from jax.experimental import pallas as pl
from jax.experimental.pallas import tpu as pltpu
from jax.sharding import PartitionSpec as P

HEAD_DIM = 128
BLOCK = 128
GROUP = 4
BLOCKS = 4
REACH_BLOCKS = 2
NEG = -1e30
VMEM_LIMIT = 40 * 1024 * 1024
LOG2E = 1.4426950408889634
MESH = pl.DeviceIdType.MESH
F32 = jnp.float32
BF16 = jnp.bfloat16


def dot(a, b, dims):
    return lax.dot_general(a, b, (dims, ((), ())), preferred_element_type=F32)


def remote(src, dst, send, recv, device):
    return pltpu.make_async_remote_copy(
        src_ref=src,
        dst_ref=dst,
        send_sem=send,
        recv_sem=recv,
        device_id=device,
        device_id_type=MESH,
    )


def kernel(
    q_ref, k_ref, v_ref, g_ref, w_ref, len_hbm, plan_hbm,
    o_ref, gi_ref, lse_ref,
    kbuf, vbuf, qbuf, gbuf, wown, wpar, dkv, leave, ret, st,
    s2, sp, sm, hp, hm, rp, rm, own, mp, mm,
    obuf, gibuf, lbuf, lout, len_ref, plan_ref,
    lsem, wsem, osem,
    halo_s, halo_r, w_s, w_r, st_s, st_r, ret_s, ret_r, lse_s, lse_r, rs_s, rs_r,
):
    n_ctx = lax.axis_size("ctx")
    n_tp = lax.axis_size("tp")
    n_y = n_tp // 2
    ctx = lax.axis_index("ctx")
    tp = lax.axis_index("tp")
    y = tp // 2
    core = tp - 2 * y
    nxt = {"ctx": lax.rem(ctx + 1, n_ctx)}
    prv = {"ctx": lax.rem(ctx + n_ctx - 1, n_ctx)}
    par = {"tp": tp + 1 - 2 * core}
    up = {"tp": lax.rem(tp + 2, n_tp)}
    dn = {"tp": lax.rem(tp + n_tp - 2, n_tp)}

    has_next = ctx < n_ctx - 1
    has_prev = ctx > 0

    def greet(device):
        pl.semaphore_signal(barrier, inc=1, device_id=device, device_id_type=MESH)

    barrier = pltpu.get_barrier_semaphore()
    pl.when(has_prev)(lambda: greet(prv))
    pl.when(has_next)(lambda: greet(nxt))
    for device in (par, up, dn):
        greet(device)
    locals_ = [
        pltpu.make_async_copy(k_ref, kbuf.at[pl.ds(256, 512)], lsem.at[0]),
        pltpu.make_async_copy(q_ref, qbuf, lsem.at[1]),
        pltpu.make_async_copy(v_ref, vbuf.at[pl.ds(256, 512)], lsem.at[2]),
        pltpu.make_async_copy(g_ref, gbuf, lsem.at[3]),
    ]
    for copy in locals_:
        copy.start()

    len_copy = pltpu.make_async_copy(len_hbm, len_ref, lsem.at[4])
    plan_copy = pltpu.make_async_copy(plan_hbm, plan_ref, lsem.at[5])
    len_copy.start()
    plan_copy.start()

    def no_halo():
        kbuf[pl.ds(0, 256), :] = jnp.zeros((256, 128), BF16)
        vbuf[pl.ds(0, 256), :] = jnp.zeros((256, 128), BF16)
        lbuf[1] = jnp.zeros((GROUP, 512), F32)

    def no_return():
        ret[...] = jnp.zeros((2, 2, 128, 128), BF16)
        lbuf[2] = jnp.zeros((GROUP, 512), F32)

    pl.when(jnp.logical_not(has_prev))(no_halo)
    pl.when(jnp.logical_not(has_next))(no_return)

    locals_[0].wait()
    locals_[2].wait()
    pl.semaphore_wait(
        barrier, 3 + jnp.where(has_next, 1, 0) + jnp.where(has_prev, 1, 0)
    )

    halo = {}
    slot = 0
    for b in (1, 0):
        for buf in (kbuf, vbuf):
            copy = remote(
                buf.at[pl.ds(512 + b * BLOCK, BLOCK)],
                buf.at[pl.ds(b * BLOCK, BLOCK)],
                halo_s.at[slot], halo_r.at[slot], nxt,
            )
            pl.when(has_next)(copy.start)
            halo.setdefault(b, []).append(copy)
            slot += 1
    def w_rows(r, c):
        return pl.ds(pl.multiple_of((2 * lax.rem(y + r, n_y) + c) * 512, 512), 512)

    w_local = [
        pltpu.make_async_copy(w_ref.at[w_rows(r, core)], wown.at[r], wsem.at[r])
        for r in range(4)
    ]
    for r in (2, 1, 3, 0):
        w_local[r].start()
    w_swap = [
        remote(w_ref.at[w_rows(r, 1 - core)], wpar.at[r], w_s.at[r], w_r.at[r], par)
        for r in range(4)
    ]
    for r in (2, 1, 3, 0):
        w_swap[r].start()

    origin = (ctx * BLOCKS - 1) * BLOCK
    len_copy.wait()

    def scan_lengths(i, carry):
        total, bits = carry
        total = total + len_ref[i]
        away = total - origin
        inside = (away >= 0) & (away <= BLOCKS * BLOCK)
        bit = jnp.left_shift(jnp.int32(1), jnp.where(inside, away // BLOCK, 0))
        return total, bits | jnp.where(inside, bit, 0)

    _, bits = lax.fori_loop(
        0,
        len_ref.shape[0],
        scan_lengths,
        (jnp.int32(0), jnp.where(ctx == 0, 2, 0).astype(jnp.int32)),
        unroll=8,
    )
    found = [jnp.bitwise_and(bits, 1 << b) for b in range(BLOCKS + 1)]

    locals_[1].wait()
    locals_[3].wait()

    scale = HEAD_DIM ** -0.5
    causal = lax.broadcasted_iota(jnp.int32, (BLOCK, BLOCK), 0) <= lax.broadcasted_iota(
        jnp.int32, (BLOCK, BLOCK), 1
    )
    causal_bias = jnp.where(causal, 0.0, NEG).astype(F32)
    causal_bias = jnp.concatenate([causal_bias] * GROUP, axis=1)
    written = set()

    def add_grad(which, index, value):
        rows = pl.ds(index * BLOCK, BLOCK)
        if (which, index) in written:
            dkv[which, rows, :] += value
        else:
            written.add((which, index))
            dkv[which, rows, :] = value

    def heads_in_rows(ref, qb):
        rows = pl.ds(qb * BLOCK, BLOCK)
        return jnp.concatenate(
            [ref[rows, pl.ds(h * HEAD_DIM, HEAD_DIM)] for h in range(GROUP)], axis=0
        )

    def bias_of(qb, block):
        if block == 2:
            return causal_bias
        edges = found[qb + 1] if block == 1 else found[qb + 1] + found[qb]
        return jnp.where(edges > 0, NEG, 0.0).astype(F32)

    exponent = scale * LOG2E

    def partial(qb, blocks, queries, grads):
        keys = kbuf[pl.ds((qb + blocks[0]) * BLOCK, len(blocks) * BLOCK), :]
        vals = vbuf[pl.ds((qb + blocks[0]) * BLOCK, len(blocks) * BLOCK), :]
        scores = dot(keys, queries, ((1,), (1,)))
        prob = dot(vals, grads, ((1,), (1,)))
        scores = jnp.concatenate(
            [
                scores[i * BLOCK : (i + 1) * BLOCK] + bias_of(qb, block)
                for i, block in enumerate(blocks)
            ],
            axis=0,
        )
        return scores, prob, jnp.max(scores, axis=0, keepdims=True)

    def begin(qb, blocks):
        queries, grads = heads_in_rows(qbuf, qb), heads_in_rows(gbuf, qb)
        scores, prob, top = partial(qb, blocks, queries, grads)
        raised = jnp.exp2((scores - top) * exponent)
        total = jnp.sum(raised, axis=0, keepdims=True)
        mixed = jnp.sum(raised * prob, axis=0, keepdims=True)
        return raised, prob, top, total, mixed

    def weigh(qb, first, known=None):
        scores, prob, top = first
        rows = pl.ds(qb * BLOCK, BLOCK)
        if known is not None:
            top = jnp.maximum(top, known[2])
        raised = jnp.exp2((scores - top) * exponent)
        total = jnp.sum(raised, axis=0, keepdims=True)
        mixed = jnp.sum(raised * prob, axis=0, keepdims=True)
        if known is not None:
            lower = jnp.exp2((known[2] - top) * exponent)
            total = total + known[3] * lower
            mixed = mixed + known[4] * lower
        inverse = 1.0 / total
        row_dot = mixed * inverse
        lse = top * scale + jnp.log(total)
        for h in range(GROUP):
            lbuf[0, pl.ds(h, 1), rows] = lse[:, h * BLOCK : (h + 1) * BLOCK]
        weights = raised * inverse
        weights_low = weights.astype(BF16)
        score_grad = (weights * (prob - row_dot)).astype(BF16)
        if known is not None:
            weights = known[0] * (lower * inverse)
            weights_low = jnp.concatenate([weights_low, weights.astype(BF16)], axis=0)
            score_grad = jnp.concatenate(
                [score_grad, (weights * (known[1] - row_dot)).astype(BF16)], axis=0
            )
        return weights_low, score_grad

    def spread(qb, weights_low, score_grad):
        rows = pl.ds(qb * BLOCK, BLOCK)
        queries, grads = heads_in_rows(qbuf, qb), heads_in_rows(gbuf, qb)
        keys = kbuf[pl.ds(qb * BLOCK, 3 * BLOCK), :]
        vals = vbuf[pl.ds(qb * BLOCK, 3 * BLOCK), :]
        key_add = dot(score_grad, queries, ((1,), (0,)))
        value_add = dot(weights_low, grads, ((1,), (0,)))
        for b in range(3):
            part = slice(b * BLOCK, (b + 1) * BLOCK)
            add_grad(0, qb + b, key_add[part])
            add_grad(1, qb + b, value_add[part])
        query_grad = (dot(keys, score_grad, ((0,), (0,))) * scale).astype(BF16)
        out = dot(vals, weights_low, ((0,), (0,))).astype(BF16)
        for h in range(GROUP):
            columns = slice(h * BLOCK, (h + 1) * BLOCK)
            st[0, qb, :, pl.ds(h * HEAD_DIM, HEAD_DIM)] = query_grad[:, columns].T
            o_ref[rows, pl.ds(h * HEAD_DIM, HEAD_DIM)] = out[:, columns].T

    def look(qb, blocks):
        return partial(qb, blocks, heads_in_rows(qbuf, qb), heads_in_rows(gbuf, qb))

    def attend(qb, blocks, known=None):
        spread(qb, *weigh(qb, look(qb, blocks), known))

    st_swap = [
        remote(st.at[0, t], st.at[1, t], st_s.at[t], st_r.at[t], par) for t in range(BLOCKS)
    ]

    back_copies = [
        remote(leave.at[b], ret.at[b], ret_s.at[b], ret_r.at[b], prv)
        for b in range(REACH_BLOCKS)
    ]

    def finish_tokens(t):
        rows = pl.ds((t + REACH_BLOCKS) * BLOCK, BLOCK)
        key_grad = dkv[0, rows, :]
        value_grad = dkv[1, rows, :]
        if t >= 2:
            pl.when(has_next)(back_copies[t - 2].wait_recv)
            key_grad = key_grad + ret[t - 2, 0].astype(F32)
            value_grad = value_grad + ret[t - 2, 1].astype(F32)
        st[0, t, :, pl.ds(GROUP * HEAD_DIM, HEAD_DIM)] = (key_grad * scale).astype(BF16)
        st[0, t, :, pl.ds((GROUP + 1) * HEAD_DIM, HEAD_DIM)] = value_grad.astype(BF16)
        st_swap[t].start()

    look2, look3 = look(2, (0, 1, 2)), look(3, (0, 1, 2))
    weigh2 = weigh(2, look2)
    weigh3 = weigh(3, look3)
    spread(2, *weigh2)
    spread(3, *weigh3)
    known1 = begin(1, (1, 2))
    known0 = begin(0, (2,))
    for copy in halo[1]:
        pl.when(has_prev)(copy.wait_recv)
    attend(1, (0,), known1)
    finish_tokens(1)
    w_local[2].wait()
    ahead = dot(st[0, 1], wown[2], ((1,), (1,)))
    for copy in halo[0]:
        pl.when(has_prev)(copy.wait_recv)
    attend(0, (0, 1), known0)
    finish_tokens(0)

    for b in range(REACH_BLOCKS):
        for which in range(2):
            leave[b, which] = dkv[which, pl.ds(b * BLOCK, BLOCK), :].astype(BF16)
        pl.when(has_prev)(back_copies[b].start)
    lse_next = remote(lbuf.at[0], lbuf.at[1], lse_s.at[0], lse_r.at[0], nxt)
    lse_prev = remote(lbuf.at[0], lbuf.at[2], lse_s.at[1], lse_r.at[1], prv)
    pl.when(has_next)(lse_next.start)
    pl.when(has_prev)(lse_prev.start)

    HALF = BLOCK // 2
    lo, hi = pl.ds(0, HALF), pl.ds(HALF, HALF)
    for r in (1, 3, 0):
        w_local[r].wait()

    sends = {}
    for t in range(BLOCKS):
        sends[t] = dict(
            h_up=remote(s2.at[t, lo], hp.at[t], rs_s.at[t, 0], rs_r.at[t, 0], up),
            h_dn=remote(s2.at[t, hi], hm.at[t], rs_s.at[t, 1], rs_r.at[t, 1], dn),
            u_up=remote(sp.at[t, hi], rp.at[t, hi], rs_s.at[t, 2], rs_r.at[t, 2], up),
            u_dn=remote(sm.at[t, lo], rm.at[t, lo], rs_s.at[t, 3], rs_r.at[t, 3], dn),
            m_up=remote(sp.at[t, lo], rp.at[t, lo], rs_s.at[t, 4], rs_r.at[t, 4], up),
            m_dn=remote(sm.at[t, hi], rm.at[t, hi], rs_s.at[t, 5], rs_r.at[t, 5], dn),
        )

    def project(t, first_time):
        st_swap[t].wait_recv()

        def part(r):
            if first_time:
                w_swap[r].wait_recv()
            mine = ahead if first_time and r == 2 else dot(st[0, t], wown[r], ((1,), (1,)))
            return mine + dot(st[1, t], wpar[r], ((1,), (1,)))

        s2[t] = part(2).astype(BF16)
        sends[t]["h_up"].start()
        sends[t]["h_dn"].start()
        piece = part(1)
        sp[t, hi, :] = piece[HALF:].astype(BF16)
        sends[t]["u_up"].start()
        mp[t] = piece[:HALF]
        piece = part(3)
        sm[t, lo, :] = piece[:HALF].astype(BF16)
        sends[t]["u_dn"].start()
        mm[t] = piece[HALF:]
        own[t] = part(0)

    def merge(t):
        sends[t]["h_up"].wait_recv()
        sp[t, lo, :] = (mp[t] + hp[t].astype(F32)).astype(BF16)
        sends[t]["m_up"].start()
        sends[t]["h_dn"].wait_recv()
        sm[t, hi, :] = (mm[t] + hm[t].astype(F32)).astype(BF16)
        sends[t]["m_dn"].start()

    def finish(t):
        for name in ("u_up", "u_dn", "m_up", "m_dn"):
            sends[t][name].wait_recv()
        rows = pl.ds(t * BLOCK, BLOCK)
        gi_ref[rows, :] = (own[t] + rp[t].astype(F32) + rm[t].astype(F32)).astype(BF16)

    project(1, True)
    project(0, False)
    merge(1)
    finish_tokens(2)
    finish_tokens(3)
    merge(0)
    project(2, False)
    project(3, False)
    merge(2)

    plan_copy.wait()
    pl.when(has_prev)(lse_next.wait_recv)
    pl.when(has_next)(lse_prev.wait_recv)
    picked = [jnp.zeros((GROUP, BLOCK), F32) for _ in range(BLOCKS)]
    rank = jnp.int32(0)
    one = jnp.int32(1)
    before, after = jnp.where(has_prev, 1, 0), jnp.where(has_next, 1, 0)
    for source, device, valid in (
        (1, prv["ctx"], before), (0, ctx, one), (2, nxt["ctx"], after),
    ):
        for b in range(BLOCKS):
            hit = jnp.where(plan_ref[device * BLOCKS + b] == ctx, valid, 0)
            piece = lbuf[source, :, pl.ds(b * BLOCK, BLOCK)]
            for s in range(BLOCKS):
                take = jnp.where((hit == 1) & (rank == s), 1.0, 0.0).astype(F32)
                picked[s] = picked[s] + piece * take
            rank = rank + hit
    for s in range(BLOCKS):
        lse_ref[:, pl.ds(s * BLOCK, BLOCK)] = picked[s]

    finish(1)
    finish(0)
    merge(3)
    finish(2)
    finish(3)

    for b in (1, 0):
        for copy in halo[b]:
            pl.when(has_next)(copy.wait_send)
    for copy in w_swap:
        copy.wait_send()
    for copy in st_swap:
        copy.wait_send()
    for copy in back_copies:
        pl.when(has_prev)(copy.wait_send)
    pl.when(has_next)(lse_next.wait_send)
    pl.when(has_prev)(lse_prev.wait_send)
    for t in range(BLOCKS):
        for copy in sends[t].values():
            copy.wait_send()


def publish(o_ref, gi_ref, lse_ref, o_out, gi_out, lse_out, sems):
    copies = [pltpu.make_async_copy(lse_ref, lse_out, sems.at[8])]
    for part in range(4):
        rows = pl.ds(part * 128, 128)
        copies.append(pltpu.make_async_copy(gi_ref.at[rows], gi_out.at[rows], sems.at[part]))
        copies.append(pltpu.make_async_copy(o_ref.at[rows], o_out.at[rows], sems.at[4 + part]))
    for copy in copies:
        copy.start()
    for copy in copies:
        copy.wait()


def body(queries, key_states, values, out_grad, weight, lengths, block_plan):
    anywhere = pl.BlockSpec(memory_space=pl.ANY)
    dma = pltpu.SemaphoreType.DMA
    shapes = (
        jax.ShapeDtypeStruct((512, 512), BF16),
        jax.ShapeDtypeStruct((512, 512), BF16),
        jax.ShapeDtypeStruct((GROUP, 512), F32),
    )
    operands = [
        pltpu.with_memory_space_constraint(operand, pltpu.HBM)
        for operand in (queries, key_states, values, out_grad, weight, lengths, block_plan)
    ]
    results = pl.pallas_call(
        kernel,
        out_shape=shapes,
        in_specs=[anywhere] * 7,
        out_specs=(pl.BlockSpec(memory_space=pltpu.VMEM),) * 3,
        scratch_shapes=[
            pltpu.VMEM((768, 128), BF16),
            pltpu.VMEM((768, 128), BF16),
            pltpu.VMEM((512, 512), BF16),
            pltpu.VMEM((512, 512), BF16),
            pltpu.VMEM((4, 512, 768), BF16),
            pltpu.VMEM((4, 512, 768), BF16),
            pltpu.VMEM((2, 768, 128), F32),
            pltpu.VMEM((2, 2, 128, 128), BF16),
            pltpu.VMEM((2, 2, 128, 128), BF16),
            pltpu.VMEM((2, 4, 128, 768), BF16),
            pltpu.VMEM((4, 128, 512), BF16),
            pltpu.VMEM((4, 128, 512), BF16),
            pltpu.VMEM((4, 128, 512), BF16),
            pltpu.VMEM((4, 64, 512), BF16),
            pltpu.VMEM((4, 64, 512), BF16),
            pltpu.VMEM((4, 128, 512), BF16),
            pltpu.VMEM((4, 128, 512), BF16),
            pltpu.VMEM((4, 128, 512), F32),
            pltpu.VMEM((4, 64, 512), F32),
            pltpu.VMEM((4, 64, 512), F32),
            pltpu.VMEM((512, 512), BF16),
            pltpu.VMEM((512, 512), BF16),
            pltpu.VMEM((3, GROUP, 512), F32),
            pltpu.VMEM((GROUP, 512), F32),
            pltpu.SMEM(lengths.shape, jnp.int32),
            pltpu.SMEM(block_plan.shape, jnp.int32),
            dma((6,)),
            dma((4,)),
            dma((6,)),
            dma((4,)), dma((4,)),
            dma((4,)), dma((4,)),
            dma((4,)), dma((4,)),
            dma((2,)), dma((2,)),
            dma((2,)), dma((2,)),
            dma((4, 6)), dma((4, 6)),
        ],
        compiler_params=pltpu.CompilerParams(
            collective_id=0, has_side_effects=True, vmem_limit_bytes=VMEM_LIMIT
        ),
    )(*operands)
    return pl.pallas_call(
        publish,
        out_shape=shapes,
        in_specs=[anywhere] * 3,
        out_specs=(anywhere,) * 3,
        scratch_shapes=[dma((9,))],
        compiler_params=pltpu.CompilerParams(vmem_limit_bytes=VMEM_LIMIT),
    )(*results)


def solution(mesh):
    in_specs = (
        P("ctx", "tp"),
        P("ctx", "tp"),
        P("ctx", "tp"),
        P("ctx", "tp"),
        P(None, "tp"),
        P(),
        P(),
    )
    out_specs = (P("ctx", "tp"), P("ctx", "tp"), P("tp", "ctx"))
    return jax.shard_map(body, mesh=mesh, in_specs=in_specs, out_specs=out_specs, check_vma=False)
```

```python
import jax
import jax.numpy as jnp
from jax import lax
from jax.experimental import pallas as pl
from jax.experimental.pallas import tpu as pltpu
from jax.sharding import PartitionSpec as P

HEAD_DIM = 128
BLOCK = 128
GROUP = 4
BLOCKS = 4
REACH_BLOCKS = 2
NEG = -1e30
VMEM_LIMIT = 40 * 1024 * 1024
LOG2E = 1.4426950408889634
MESH = pl.DeviceIdType.MESH
F32 = jnp.float32
BF16 = jnp.bfloat16


def dot(a, b, dims):
    return lax.dot_general(a, b, (dims, ((), ())), preferred_element_type=F32)


def remote(src, dst, send, recv, device):
    return pltpu.make_async_remote_copy(
        src_ref=src,
        dst_ref=dst,
        send_sem=send,
        recv_sem=recv,
        device_id=device,
        device_id_type=MESH,
    )


def kernel(
    q_ref, k_ref, v_ref, g_ref, w_ref, len_hbm, plan_hbm,
    o_ref, gi_ref, lse_ref,
    kbuf, vbuf, qbuf, gbuf, wown, wpar, dkv, leave, ret, st,
    s2, sp, sm, hp, hm, rp, rm, own, mp, mm,
    obuf, gibuf, lbuf, lout, len_ref, plan_ref,
    lsem, wsem, osem,
    halo_s, halo_r, w_s, w_r, st_s, st_r, ret_s, ret_r, lse_s, lse_r, rs_s, rs_r,
):
    n_ctx = lax.axis_size("ctx")
    n_tp = lax.axis_size("tp")
    n_y = n_tp // 2
    ctx = lax.axis_index("ctx")
    tp = lax.axis_index("tp")
    y = tp // 2
    core = tp - 2 * y
    nxt = {"ctx": lax.rem(ctx + 1, n_ctx)}
    prv = {"ctx": lax.rem(ctx + n_ctx - 1, n_ctx)}
    par = {"tp": tp + 1 - 2 * core}
    up = {"tp": lax.rem(tp + 2, n_tp)}
    dn = {"tp": lax.rem(tp + n_tp - 2, n_tp)}

    has_next = ctx < n_ctx - 1
    has_prev = ctx > 0

    def greet(device):
        pl.semaphore_signal(barrier, inc=1, device_id=device, device_id_type=MESH)

    barrier = pltpu.get_barrier_semaphore()
    pl.when(has_prev)(lambda: greet(prv))
    pl.when(has_next)(lambda: greet(nxt))
    for device in (par, up, dn):
        greet(device)
    locals_ = [
        pltpu.make_async_copy(k_ref, kbuf.at[pl.ds(256, 512)], lsem.at[0]),
        pltpu.make_async_copy(q_ref, qbuf, lsem.at[1]),
        pltpu.make_async_copy(v_ref, vbuf.at[pl.ds(256, 512)], lsem.at[2]),
        pltpu.make_async_copy(g_ref, gbuf, lsem.at[3]),
    ]
    for copy in locals_:
        copy.start()

    len_copy = pltpu.make_async_copy(len_hbm, len_ref, lsem.at[4])
    plan_copy = pltpu.make_async_copy(plan_hbm, plan_ref, lsem.at[5])
    len_copy.start()
    plan_copy.start()

    def no_halo():
        kbuf[pl.ds(0, 256), :] = jnp.zeros((256, 128), BF16)
        vbuf[pl.ds(0, 256), :] = jnp.zeros((256, 128), BF16)
        lbuf[1] = jnp.zeros((GROUP, 512), F32)

    def no_return():
        ret[...] = jnp.zeros((2, 2, 128, 128), BF16)
        lbuf[2] = jnp.zeros((GROUP, 512), F32)

    pl.when(jnp.logical_not(has_prev))(no_halo)
    pl.when(jnp.logical_not(has_next))(no_return)

    locals_[0].wait()
    locals_[2].wait()
    pl.semaphore_wait(
        barrier, 3 + jnp.where(has_next, 1, 0) + jnp.where(has_prev, 1, 0)
    )

    halo = {}
    slot = 0
    for b in (1, 0):
        for buf in (kbuf, vbuf):
            copy = remote(
                buf.at[pl.ds(512 + b * BLOCK, BLOCK)],
                buf.at[pl.ds(b * BLOCK, BLOCK)],
                halo_s.at[slot], halo_r.at[slot], nxt,
            )
            pl.when(has_next)(copy.start)
            halo.setdefault(b, []).append(copy)
            slot += 1
    def w_rows(r, c):
        return pl.ds(pl.multiple_of((2 * lax.rem(y + r, n_y) + c) * 512, 512), 512)

    w_local = [
        pltpu.make_async_copy(w_ref.at[w_rows(r, core)], wown.at[r], wsem.at[r])
        for r in range(4)
    ]
    for r in (2, 1, 3, 0):
        w_local[r].start()
    w_swap = [
        remote(w_ref.at[w_rows(r, 1 - core)], wpar.at[r], w_s.at[r], w_r.at[r], par)
        for r in range(4)
    ]
    for r in (2, 1, 3, 0):
        w_swap[r].start()

    origin = (ctx * BLOCKS - 1) * BLOCK
    len_copy.wait()

    def scan_lengths(i, carry):
        total, bits = carry
        total = total + len_ref[i]
        away = total - origin
        inside = (away >= 0) & (away <= BLOCKS * BLOCK)
        bit = jnp.left_shift(jnp.int32(1), jnp.where(inside, away // BLOCK, 0))
        return total, bits | jnp.where(inside, bit, 0)

    _, bits = lax.fori_loop(
        0,
        len_ref.shape[0],
        scan_lengths,
        (jnp.int32(0), jnp.where(ctx == 0, 2, 0).astype(jnp.int32)),
        unroll=8,
    )
    found = [jnp.bitwise_and(bits, 1 << b) for b in range(BLOCKS + 1)]

    locals_[1].wait()
    locals_[3].wait()

    scale = HEAD_DIM ** -0.5
    causal = lax.broadcasted_iota(jnp.int32, (BLOCK, BLOCK), 0) <= lax.broadcasted_iota(
        jnp.int32, (BLOCK, BLOCK), 1
    )
    causal_bias = jnp.where(causal, 0.0, NEG).astype(F32)
    causal_bias = jnp.concatenate([causal_bias] * GROUP, axis=1)
    written = set()

    def add_grad(which, index, value):
        rows = pl.ds(index * BLOCK, BLOCK)
        if (which, index) in written:
            dkv[which, rows, :] += value
        else:
            written.add((which, index))
            dkv[which, rows, :] = value

    def heads_in_rows(ref, qb):
        rows = pl.ds(qb * BLOCK, BLOCK)
        return jnp.concatenate(
            [ref[rows, pl.ds(h * HEAD_DIM, HEAD_DIM)] for h in range(GROUP)], axis=0
        )

    def bias_of(qb, block):
        if block == 2:
            return causal_bias
        edges = found[qb + 1] if block == 1 else found[qb + 1] + found[qb]
        return jnp.where(edges > 0, NEG, 0.0).astype(F32)

    exponent = scale * LOG2E

    def partial(qb, blocks, queries, grads):
        keys = kbuf[pl.ds((qb + blocks[0]) * BLOCK, len(blocks) * BLOCK), :]
        vals = vbuf[pl.ds((qb + blocks[0]) * BLOCK, len(blocks) * BLOCK), :]
        scores = dot(keys, queries, ((1,), (1,)))
        prob = dot(vals, grads, ((1,), (1,)))
        scores = jnp.concatenate(
            [
                scores[i * BLOCK : (i + 1) * BLOCK] + bias_of(qb, block)
                for i, block in enumerate(blocks)
            ],
            axis=0,
        )
        return scores, prob, jnp.max(scores, axis=0, keepdims=True)

    def begin(qb, blocks):
        queries, grads = heads_in_rows(qbuf, qb), heads_in_rows(gbuf, qb)
        scores, prob, top = partial(qb, blocks, queries, grads)
        raised = jnp.exp2((scores - top) * exponent)
        total = jnp.sum(raised, axis=0, keepdims=True)
        mixed = jnp.sum(raised * prob, axis=0, keepdims=True)
        return raised, prob, top, total, mixed

    def weigh(qb, first, known=None):
        scores, prob, top = first
        rows = pl.ds(qb * BLOCK, BLOCK)
        if known is not None:
            top = jnp.maximum(top, known[2])
        raised = jnp.exp2((scores - top) * exponent)
        total = jnp.sum(raised, axis=0, keepdims=True)
        mixed = jnp.sum(raised * prob, axis=0, keepdims=True)
        if known is not None:
            lower = jnp.exp2((known[2] - top) * exponent)
            total = total + known[3] * lower
            mixed = mixed + known[4] * lower
        inverse = 1.0 / total
        row_dot = mixed * inverse
        lse = top * scale + jnp.log(total)
        for h in range(GROUP):
            lbuf[0, pl.ds(h, 1), rows] = lse[:, h * BLOCK : (h + 1) * BLOCK]
        weights = raised * inverse
        weights_low = weights.astype(BF16)
        score_grad = (weights * (prob - row_dot)).astype(BF16)
        if known is not None:
            weights = known[0] * (lower * inverse)
            weights_low = jnp.concatenate([weights_low, weights.astype(BF16)], axis=0)
            score_grad = jnp.concatenate(
                [score_grad, (weights * (known[1] - row_dot)).astype(BF16)], axis=0
            )
        return weights_low, score_grad

    def spread(qb, weights_low, score_grad):
        rows = pl.ds(qb * BLOCK, BLOCK)
        queries, grads = heads_in_rows(qbuf, qb), heads_in_rows(gbuf, qb)
        keys = kbuf[pl.ds(qb * BLOCK, 3 * BLOCK), :]
        vals = vbuf[pl.ds(qb * BLOCK, 3 * BLOCK), :]
        key_add = dot(score_grad, queries, ((1,), (0,)))
        value_add = dot(weights_low, grads, ((1,), (0,)))
        for b in range(3):
            part = slice(b * BLOCK, (b + 1) * BLOCK)
            add_grad(0, qb + b, key_add[part])
            add_grad(1, qb + b, value_add[part])
        query_grad = (dot(keys, score_grad, ((0,), (0,))) * scale).astype(BF16)
        out = dot(vals, weights_low, ((0,), (0,))).astype(BF16)
        for h in range(GROUP):
            columns = slice(h * BLOCK, (h + 1) * BLOCK)
            st[0, qb, :, pl.ds(h * HEAD_DIM, HEAD_DIM)] = query_grad[:, columns].T
            o_ref[rows, pl.ds(h * HEAD_DIM, HEAD_DIM)] = out[:, columns].T

    def look(qb, blocks):
        return partial(qb, blocks, heads_in_rows(qbuf, qb), heads_in_rows(gbuf, qb))

    def attend(qb, blocks, known=None):
        spread(qb, *weigh(qb, look(qb, blocks), known))

    st_swap = [
        remote(st.at[0, t], st.at[1, t], st_s.at[t], st_r.at[t], par) for t in range(BLOCKS)
    ]

    back_copies = [
        remote(leave.at[b], ret.at[b], ret_s.at[b], ret_r.at[b], prv)
        for b in range(REACH_BLOCKS)
    ]

    def finish_tokens(t):
        rows = pl.ds((t + REACH_BLOCKS) * BLOCK, BLOCK)
        key_grad = dkv[0, rows, :]
        value_grad = dkv[1, rows, :]
        if t >= 2:
            pl.when(has_next)(back_copies[t - 2].wait_recv)
            key_grad = key_grad + ret[t - 2, 0].astype(F32)
            value_grad = value_grad + ret[t - 2, 1].astype(F32)
        st[0, t, :, pl.ds(GROUP * HEAD_DIM, HEAD_DIM)] = (key_grad * scale).astype(BF16)
        st[0, t, :, pl.ds((GROUP + 1) * HEAD_DIM, HEAD_DIM)] = value_grad.astype(BF16)
        st_swap[t].start()

    look2, look3 = look(2, (0, 1, 2)), look(3, (0, 1, 2))
    weigh2 = weigh(2, look2)
    weigh3 = weigh(3, look3)
    spread(2, *weigh2)
    spread(3, *weigh3)
    known1 = begin(1, (1, 2))
    known0 = begin(0, (2,))
    for copy in halo[1]:
        pl.when(has_prev)(copy.wait_recv)
    attend(1, (0,), known1)
    finish_tokens(1)
    w_local[2].wait()
    ahead = dot(st[0, 1], wown[2], ((1,), (1,)))
    for copy in halo[0]:
        pl.when(has_prev)(copy.wait_recv)
    attend(0, (0, 1), known0)
    finish_tokens(0)

    for b in range(REACH_BLOCKS):
        for which in range(2):
            leave[b, which] = dkv[which, pl.ds(b * BLOCK, BLOCK), :].astype(BF16)
        pl.when(has_prev)(back_copies[b].start)
    lse_next = remote(lbuf.at[0], lbuf.at[1], lse_s.at[0], lse_r.at[0], nxt)
    lse_prev = remote(lbuf.at[0], lbuf.at[2], lse_s.at[1], lse_r.at[1], prv)

    HALF = BLOCK // 2
    lo, hi = pl.ds(0, HALF), pl.ds(HALF, HALF)
    for r in (1, 3, 0):
        w_local[r].wait()

    sends = {}
    for t in range(BLOCKS):
        sends[t] = dict(
            h_up=remote(s2.at[t, lo], hp.at[t], rs_s.at[t, 0], rs_r.at[t, 0], up),
            h_dn=remote(s2.at[t, hi], hm.at[t], rs_s.at[t, 1], rs_r.at[t, 1], dn),
            u_up=remote(sp.at[t, hi], rp.at[t, hi], rs_s.at[t, 2], rs_r.at[t, 2], up),
            u_dn=remote(sm.at[t, lo], rm.at[t, lo], rs_s.at[t, 3], rs_r.at[t, 3], dn),
            m_up=remote(sp.at[t, lo], rp.at[t, lo], rs_s.at[t, 4], rs_r.at[t, 4], up),
            m_dn=remote(sm.at[t, hi], rm.at[t, hi], rs_s.at[t, 5], rs_r.at[t, 5], dn),
        )

    def project(t, first_time, hold=False):
        st_swap[t].wait_recv()

        def part(r):
            if first_time:
                w_swap[r].wait_recv()
            mine = ahead if first_time and r == 2 else dot(st[0, t], wown[r], ((1,), (1,)))
            return mine + dot(st[1, t], wpar[r], ((1,), (1,)))

        s2[t] = part(2).astype(BF16)
        sends[t]["h_up"].start()
        sends[t]["h_dn"].start()
        piece = part(1)
        sp[t, hi, :] = piece[HALF:].astype(BF16)
        if not hold:
            sends[t]["u_up"].start()
        mp[t] = piece[:HALF]
        piece = part(3)
        sm[t, lo, :] = piece[:HALF].astype(BF16)
        if not hold:
            sends[t]["u_dn"].start()
        mm[t] = piece[HALF:]

    def keep(t, first_time=False):
        if first_time:
            w_swap[0].wait_recv()
        own[t] = dot(st[0, t], wown[0], ((1,), (1,))) + dot(st[1, t], wpar[0], ((1,), (1,)))

    def release(t):
        sends[t]["u_up"].start()
        sends[t]["u_dn"].start()

    def merge(t):
        sends[t]["h_up"].wait_recv()
        sp[t, lo, :] = (mp[t] + hp[t].astype(F32)).astype(BF16)
        sends[t]["m_up"].start()
        sends[t]["h_dn"].wait_recv()
        sm[t, hi, :] = (mm[t] + hm[t].astype(F32)).astype(BF16)
        sends[t]["m_dn"].start()

    def finish(t):
        for name in ("u_up", "u_dn", "m_up", "m_dn"):
            sends[t][name].wait_recv()
        rows = pl.ds(t * BLOCK, BLOCK)
        gi_ref[rows, :] = (own[t] + rp[t].astype(F32) + rm[t].astype(F32)).astype(BF16)

    project(1, True)
    pl.when(has_next)(lse_next.start)
    pl.when(has_prev)(lse_prev.start)
    project(0, False, True)
    merge(1)
    release(0)
    finish_tokens(2)
    finish_tokens(3)
    keep(1, True)
    merge(0)
    keep(0)
    project(2, False, True)
    project(3, False, True)
    merge(2)
    release(2)
    release(3)
    keep(2)
    keep(3)

    plan_copy.wait()
    pl.when(has_prev)(lse_next.wait_recv)
    pl.when(has_next)(lse_prev.wait_recv)
    picked = [jnp.zeros((GROUP, BLOCK), F32) for _ in range(BLOCKS)]
    rank = jnp.int32(0)
    one = jnp.int32(1)
    before, after = jnp.where(has_prev, 1, 0), jnp.where(has_next, 1, 0)
    for source, device, valid in (
        (1, prv["ctx"], before), (0, ctx, one), (2, nxt["ctx"], after),
    ):
        for b in range(BLOCKS):
            hit = jnp.where(plan_ref[device * BLOCKS + b] == ctx, valid, 0)
            piece = lbuf[source, :, pl.ds(b * BLOCK, BLOCK)]
            for s in range(BLOCKS):
                take = jnp.where((hit == 1) & (rank == s), 1.0, 0.0).astype(F32)
                picked[s] = picked[s] + piece * take
            rank = rank + hit
    for s in range(BLOCKS):
        lse_ref[:, pl.ds(s * BLOCK, BLOCK)] = picked[s]

    finish(1)
    finish(0)
    merge(3)
    finish(2)
    finish(3)

    for b in (1, 0):
        for copy in halo[b]:
            pl.when(has_next)(copy.wait_send)
    for copy in w_swap:
        copy.wait_send()
    for copy in st_swap:
        copy.wait_send()
    for copy in back_copies:
        pl.when(has_prev)(copy.wait_send)
    pl.when(has_next)(lse_next.wait_send)
    pl.when(has_prev)(lse_prev.wait_send)
    for t in range(BLOCKS):
        for copy in sends[t].values():
            copy.wait_send()


def publish(o_ref, gi_ref, lse_ref, o_out, gi_out, lse_out, sems):
    copies = [pltpu.make_async_copy(lse_ref, lse_out, sems.at[8])]
    for part in range(4):
        rows = pl.ds(part * 128, 128)
        copies.append(pltpu.make_async_copy(gi_ref.at[rows], gi_out.at[rows], sems.at[part]))
        copies.append(pltpu.make_async_copy(o_ref.at[rows], o_out.at[rows], sems.at[4 + part]))
    for copy in copies:
        copy.start()
    for copy in copies:
        copy.wait()


def body(queries, key_states, values, out_grad, weight, lengths, block_plan):
    anywhere = pl.BlockSpec(memory_space=pl.ANY)
    dma = pltpu.SemaphoreType.DMA
    shapes = (
        jax.ShapeDtypeStruct((512, 512), BF16),
        jax.ShapeDtypeStruct((512, 512), BF16),
        jax.ShapeDtypeStruct((GROUP, 512), F32),
    )
    operands = [
        pltpu.with_memory_space_constraint(operand, pltpu.HBM)
        for operand in (queries, key_states, values, out_grad, weight, lengths, block_plan)
    ]
    results = pl.pallas_call(
        kernel,
        out_shape=shapes,
        in_specs=[anywhere] * 7,
        out_specs=(pl.BlockSpec(memory_space=pltpu.VMEM),) * 3,
        scratch_shapes=[
            pltpu.VMEM((768, 128), BF16),
            pltpu.VMEM((768, 128), BF16),
            pltpu.VMEM((512, 512), BF16),
            pltpu.VMEM((512, 512), BF16),
            pltpu.VMEM((4, 512, 768), BF16),
            pltpu.VMEM((4, 512, 768), BF16),
            pltpu.VMEM((2, 768, 128), F32),
            pltpu.VMEM((2, 2, 128, 128), BF16),
            pltpu.VMEM((2, 2, 128, 128), BF16),
            pltpu.VMEM((2, 4, 128, 768), BF16),
            pltpu.VMEM((4, 128, 512), BF16),
            pltpu.VMEM((4, 128, 512), BF16),
            pltpu.VMEM((4, 128, 512), BF16),
            pltpu.VMEM((4, 64, 512), BF16),
            pltpu.VMEM((4, 64, 512), BF16),
            pltpu.VMEM((4, 128, 512), BF16),
            pltpu.VMEM((4, 128, 512), BF16),
            pltpu.VMEM((4, 128, 512), F32),
            pltpu.VMEM((4, 64, 512), F32),
            pltpu.VMEM((4, 64, 512), F32),
            pltpu.VMEM((512, 512), BF16),
            pltpu.VMEM((512, 512), BF16),
            pltpu.VMEM((3, GROUP, 512), F32),
            pltpu.VMEM((GROUP, 512), F32),
            pltpu.SMEM(lengths.shape, jnp.int32),
            pltpu.SMEM(block_plan.shape, jnp.int32),
            dma((6,)),
            dma((4,)),
            dma((6,)),
            dma((4,)), dma((4,)),
            dma((4,)), dma((4,)),
            dma((4,)), dma((4,)),
            dma((2,)), dma((2,)),
            dma((2,)), dma((2,)),
            dma((4, 6)), dma((4, 6)),
        ],
        compiler_params=pltpu.CompilerParams(
            collective_id=0, has_side_effects=True, vmem_limit_bytes=VMEM_LIMIT
        ),
    )(*operands)
    return pl.pallas_call(
        publish,
        out_shape=shapes,
        in_specs=[anywhere] * 3,
        out_specs=(anywhere,) * 3,
        scratch_shapes=[dma((9,))],
        compiler_params=pltpu.CompilerParams(vmem_limit_bytes=VMEM_LIMIT),
    )(*results)


def solution(mesh):
    in_specs = (
        P("ctx", "tp"),
        P("ctx", "tp"),
        P("ctx", "tp"),
        P("ctx", "tp"),
        P(None, "tp"),
        P(),
        P(),
    )
    out_specs = (P("ctx", "tp"), P("ctx", "tp"), P("tp", "ctx"))
    return jax.shard_map(body, mesh=mesh, in_specs=in_specs, out_specs=out_specs, check_vma=False)
```
